512 devices in a mesh: rank: 8 (over z_hi, x), fsdp: 64 (over y, z_lo, core).
Axes of the slice: x: 4, y: 8, z: 8 (z_hi: 2, z_lo: 4; z = z_hi * 4 + z_lo), core: 2. Of those that a mesh axis runs over, the one named last changes fastest.
Arguments:
- cotangents: bfloat16 [8192, 8192], P('fsdp', 'rank'), may hold values from -0.25 to 0.25
- hidden: bfloat16 [8192, 14336], P('fsdp'), may hold values from -6 to 6
- projector: bfloat16 [8192, 2048], P('rank', 'fsdp'), may hold values from -0.0625 to 0.0625
- moment_first: bfloat16 [2048, 14336], P('rank', 'fsdp'), may hold values from -3 to 3
- moment_second: bfloat16 [2048, 14336], P('rank', 'fsdp'), may hold values from 0.0039978027 to 0.3984375
Outputs:
- update: bfloat16 [8192, 14336], P('rank', 'fsdp')
- first_moment: bfloat16 [2048, 14336], P('rank', 'fsdp')
- second_moment: bfloat16 [2048, 14336], P('rank', 'fsdp')
The draws below stay inside these ranges and needn't reach their ends.
All inputs are finite; a program needn't handle non-finite values.
Results may differ from the reference program's by a relative error of at most 0.019.
Values may be sent and summed in bfloat16 or wider, within the bound.
A program may use at most 64 MiB of HBM per device.

```python
import math
import jax
import jax.numpy as jnp

D = 8192
FW = 14336
RANK = 2048
STEP = 20
TOKENS = 8192


def block_scale(stream_key, extent, pieces, least, top_value):
    loudness = 1.0
    for position, parts in pieces:
        draws = jax.random.uniform(jax.random.fold_in(jax.random.fold_in(stream_key, 6), position), (parts,), jnp.float32, least / len(pieces), top_value / len(pieces))
        loudness = loudness * jnp.repeat(jnp.exp(draws), extent[position] // parts).reshape((-1,) + (1,) * (len(extent) - 1 - position))
    return loudness


def gaussian(own_key, dims, deviation, most, pieces=(), kind=jnp.bfloat16):
    values = deviation * jax.random.normal(own_key, dims, jnp.float32)
    if pieces:
        values = values * block_scale(own_key, dims, pieces, -0.22, 0.18)
    return jnp.clip(values, -most, most).astype(kind)


def setup_inputs(seed: int = 0) -> dict:
    splits = jax.random.split(jax.random.key(seed), 6)
    return {
        "cotangents": gaussian(splits[0], (TOKENS, D), (4 * TOKENS ** -0.5), 0.25, ((0, 64), (1, 8))),
        "hidden": gaussian(splits[1], (TOKENS, FW), 1.0, 6.0, ((0, 64),)),
        "projector": gaussian(splits[2], (D, RANK), D ** -0.5, 0.0625, ((0, 8), (1, 64))),
        "moment_first": gaussian(splits[3], (RANK, FW), 0.5, 3.0, ((0, 8), (1, 64))),
        "moment_second": jnp.clip(jnp.exp(math.log(0.3984375) - 4.6018058 * jax.random.uniform(splits[4], (RANK, FW), jnp.float32) ** block_scale(splits[4], (RANK, FW), ((0, 8), (1, 64)), -0.2, 0.2)), 0.0039978027, 0.3984375).astype(jnp.bfloat16),
    }


def reference(cotangents, hidden, projector, moment_first, moment_second):
    left_factor = jnp.dot(cotangents, projector, preferred_element_type=jnp.float32).astype(jnp.bfloat16)
    projected = jnp.dot(left_factor.T, hidden, preferred_element_type=jnp.float32)
    first_f = 0.9 * moment_first.astype(jnp.float32) + 0.1 * projected
    second_f = 0.999 * moment_second.astype(jnp.float32) + 0.001 * projected * projected
    first_fix = 1.0 - 0.9 ** STEP
    second_fix = 1.0 - 0.999 ** STEP
    direction = (first_f / first_fix / (jnp.sqrt(second_f / second_fix) + 1e-08)).astype(jnp.bfloat16)
    update = jnp.dot(projector, direction, preferred_element_type=jnp.float32).astype(jnp.bfloat16)
    return (update, first_f.astype(jnp.bfloat16), second_f.astype(jnp.bfloat16))
```

```python
import jax
import jax.numpy as jnp
from jax import lax
from jax.experimental import pallas as pl
from jax.experimental.pallas import tpu as pltpu
from jax.sharding import PartitionSpec as P

STEP = 20
FIRST_FIX = 1.0 - 0.9**STEP
SECOND_FIX = 1.0 - 0.999**STEP
BF = jnp.bfloat16
F32 = jnp.float32
MESH = pl.DeviceIdType.MESH
ORDER = (4, 3, 5, 2, 6, 1, 7, 0)
OWNER = {4: (0, 0), 3: (0, 1), 5: (0, 2), 2: (0, 3), 0: (1, 0), 7: (1, 1), 1: (1, 2), 6: (1, 3)}


def body(
    cot, hid, prj, mom1, mom2,
    upd, new1, new2,
    hid_v, hid_t, hbuf, p_t, cot_t, xs, xb, zs, zb, lt, lt2, part, stage, arrived, dr, m1t, m2t, pad,
    loc_sem,
    pp_s, pp_r, ct_s, ct_r, ring_s, ring_r, hz_s, hz_r, hx_s, hx_r, hs_s, hs_r,
    ls_s, ls_r, lz_s, lz_r, lg_s, lg_r, lc_s, lc_r, p2_s, p2_r, pc_s, pc_r,
    rs_s, rs_r, dz_s, dz_r, dx_s, dx_r,
):
    rank = lax.axis_index("rank")
    shard = lax.axis_index("fsdp")
    zh, x = rank // 4, rank % 4
    y, zl, c = shard // 8, (shard // 2) % 4, shard % 2
    z = zh * 4 + zl
    low, high, pair = zl % 2, zl // 2, zl // 2

    def at(zh_, x_, y_, zl_, c_):
        return (zh_ * 4 + x_, y_ * 8 + zl_ * 2 + c_)

    def at_z(z_, c_):
        return at(z_ // 4, x, y, z_ % 4, c_)

    def rcopy(src, dst, ssem, rsem, dev):
        return pltpu.make_async_remote_copy(
            src_ref=src, dst_ref=dst, send_sem=ssem, recv_sem=rsem, device_id=dev, device_id_type=MESH
        )

    sibling = at(zh, x, y, zl, 1 - c)
    partner = at(1 - zh, x, y, zl, c)
    up, down = at(zh, x, (y + 1) % 8, zl, c), at(zh, x, (y + 7) % 8, zl, c)
    xpeers = [((x + k) % 4, at(zh, (x + k) % 4, y, zl, c)) for k in (1, 2, 3)]
    zpeers = [((zl + k) % 4, at(zh, x, y, (zl + k) % 4, c)) for k in (1, 2, 3)]

    load = pltpu.make_async_copy(hid, hid_v, loc_sem.at[0])
    load.start()

    own_lane = pl.multiple_of(low * 256 + c * 128, 128)
    own_rows = pl.multiple_of(high * 32, 32)
    other_rows = pl.multiple_of((1 - high) * 32, 32)
    p_t[y, low, c, pl.ds(own_rows, 32), :] = prj[...].T
    cot_t[:, pl.ds(own_lane, 128)] = cot[...].T

    barrier = pltpu.get_barrier_semaphore()
    greet = [sibling, partner, up, down] + [d for _, d in xpeers] + [d for _, d in zpeers]
    for off in (1, 7, 2, 6):
        for cc in (0, 1):
            greet.append(at_z((z + off) % 8, cc))
    for dev in greet:
        pl.semaphore_signal(barrier, inc=1, device_id=dev, device_id_type=MESH)
    pl.semaphore_wait(barrier, len(greet))

    sends = []

    pp = rcopy(
        p_t.at[y, low, c, pl.ds(own_rows, 32)], p_t.at[y, low, c, pl.ds(own_rows, 32)],
        pp_s, pp_r, at(zh, x, y, (zl + 2) % 4, c),
    )
    pp.start()
    pp_in = rcopy(
        p_t.at[y, low, c, pl.ds(other_rows, 32)], p_t.at[y, low, c, pl.ds(other_rows, 32)],
        pp_s, pp_r, at(zh, x, y, (zl + 2) % 4, c),
    )

    def ring(direction, h, step, incoming=False):
        back = step + (1 if incoming else 0)
        origin = (y + 8 - back) % 8 if direction == 0 else (y + back) % 8
        rows = pl.multiple_of(h * 32, 32)
        ref = p_t.at[origin, low, c, pl.ds(rows, 32)]
        return rcopy(
            ref, ref, ring_s.at[direction, h, step], ring_r.at[direction, h, step], up if direction == 0 else down
        )

    ring(0, high, 0).start()
    ring(1, high, 0).start()

    ct = [
        rcopy(cot_t.at[:, pl.ds(own_lane, 128)], cot_t.at[:, pl.ds(own_lane, 128)], ct_s.at[0], ct_r.at[0],
              at(zh, x, y, zl + 1 - 2 * low, c)),
        rcopy(cot_t.at[:, pl.ds(own_lane, 128)], cot_t.at[:, pl.ds(own_lane, 128)], ct_s.at[1], ct_r.at[1], sibling),
    ]
    for copy in ct:
        copy.start()

    def transpose_block(block):
        def tile(t, carry):
            column = pl.multiple_of(block * 1792 + t * 128, 128)
            row = pl.multiple_of(t * 128, 128)
            hid_t[block, pl.ds(row, 128), :] = hid_v[:, pl.ds(column, 128)].T
            return carry

        lax.fori_loop(0, 14, tile, 0, unroll=7)

    first = jnp.where(x == 0, 4, jnp.where(x == 1, 3, jnp.where(x == 2, 5, 2)))
    blocks = [(y + first) % 8, (y + first + 4) % 8]

    def hidden_sends(rnd):
        out = []
        block = blocks[rnd]
        for k, (off, rot) in enumerate(((1, 3), (7, 1), (None, 2))):
            zd = (z + off) % 8 if off is not None else (z + 2 + 4 * c) % 8
            lane = pl.multiple_of(rot * 256 + c * 128, 128)
            for cc in (0, 1):
                row = pl.multiple_of((2 * (zd % 4) + cc) * 224, 16)
                out.append(rcopy(
                    hid_t.at[block, pl.ds(row, 224)], hbuf.at[block, :, pl.ds(lane, 128)],
                    hz_s.at[rnd, k, cc], hz_r.at[rnd, 2 * k + c], at_z(zd, cc),
                ))
        return out

    def hidden_wait(rnd):
        block = blocks[rnd]
        for k, rot in enumerate((3, 1, 2)):
            for cc in (0, 1):
                lane = rot * 256 + cc * 128
                ref = hbuf.at[block, :, pl.ds(lane, 128)]
                rcopy(ref, ref, hz_s.at[rnd, k, cc], hz_r.at[rnd, 2 * k + cc], sibling).wait_recv()

    def hidden_forward(rnd):
        ref = hbuf.at[blocks[rnd], :, pl.ds(256, 768)]
        return [
            rcopy(ref, ref, hx_s.at[rnd, k], hx_r.at[rnd, x], dev) for k, (_, dev) in enumerate(xpeers)
        ]

    load.wait()
    hz = []
    for rnd in (0, 1):
        transpose_block(blocks[rnd])
        copies = hidden_sends(rnd)
        for copy in copies:
            copy.start()
        hz += copies

    pp_in.wait_recv()
    ring(0, 1 - high, 0).start()
    ring(1, 1 - high, 0).start()

    other_lane = pl.multiple_of((1 - low) * 256 + c * 128, 128)
    ct_in = rcopy(cot_t.at[:, pl.ds(other_lane, 128)], cot_t.at[:, pl.ds(other_lane, 128)], ct_s.at[0], ct_r.at[0], sibling)
    ct_in.wait_recv()
    ct.append(rcopy(cot_t.at[:, pl.ds(other_lane, 128)], cot_t.at[:, pl.ds(other_lane, 128)], ct_s.at[2], ct_r.at[2], sibling))
    ct[2].start()
    for k, lo in ((1, low), (2, 1 - low)):
        lane = pl.multiple_of(lo * 256 + (1 - c) * 128, 128)
        ref = cot_t.at[:, pl.ds(lane, 128)]
        rcopy(ref, ref, ct_s.at[k], ct_r.at[k], sibling).wait_recv()

    def left_copy(block):
        return rcopy(
            xs.at[block], xb.at[x, block // 4], ls_s.at[block], ls_r.at[x, block // 4], at(zh, block % 4, y, zl, c)
        )

    def left_block(block):
        xs[block] = jnp.dot(p_t[block, low, c], cot_t[...], preferred_element_type=F32).astype(BF)

        @pl.when(block % 4 != x)
        def _():
            left_copy(block).start()

    left_block(y)
    hx = []
    for step in range(4):
        for direction, h in ((0, 0), (1, 1), (0, 1), (1, 0)):
            if step == 3 and direction != h:
                continue
            ring(direction, h, step, incoming=True).wait_recv()
            if step < 2 or (step == 2 and direction == h):
                ring(direction, h, step + 1).start()
        if step < 3:
            left_block((y + 7 - step) % 8)
            left_block((y + 1 + step) % 8)
        else:
            left_block((y + 4) % 8)
        if step == 0:
            for k in range(1, 4):
                transpose_block((blocks[0] + k) % 8)
        if step == 1:
            for k in range(5, 8):
                transpose_block((blocks[0] + k) % 8)
            hidden_wait(0)
            copies = hidden_forward(0)
            for copy in copies:
                copy.start()
            hx += copies
        if step == 2:
            own = pltpu.make_async_copy(
                hid_t.at[:, pl.ds(pl.multiple_of((2 * zl + c) * 224, 16), 224)],
                hbuf.at[:, :, pl.ds(pl.multiple_of(c * 128, 128), 128)],
                loc_sem.at[1],
            )
            own.start()
            hs = rcopy(
                hid_t.at[:, pl.ds(pl.multiple_of((2 * zl + 1 - c) * 224, 16), 224)],
                hbuf.at[:, :, pl.ds(pl.multiple_of(c * 128, 128), 128)],
                hs_s, hs_r, sibling,
            )
            hs.start()

    def left_wait(half):
        for sx, _ in xpeers:
            ref = xb.at[sx, half]
            rcopy(ref, ref, ls_s.at[0], ls_r.at[sx, half], sibling).wait_recv()

    def left_sum(half):
        total = xs[half * 4 + x].astype(F32)
        for sx, _ in xpeers:
            total = total + xb[sx, half].astype(F32)
        return total

    left_wait(1 - zh)
    zs[...] = left_sum(1 - zh).astype(BF)
    lz = rcopy(zs, zb, lz_s, lz_r, partner)
    lz.start()
    hidden_wait(1)
    copies = hidden_forward(1)
    for copy in copies:
        copy.start()
    hx += copies
    for src, dst in ((mom1, m1t), (mom2, m2t)):
        pad[...] = jnp.zeros_like(pad)
        pad[:, :224] = src[...].astype(F32)
        dst[...] = pad[...].T[:224, :]
    left_wait(zh)
    lz.wait_recv()
    lt[pair, low, c] = (left_sum(zh) + zb[...].astype(F32)).astype(BF)

    mine = lt.at[pair, low, c]
    lg = [rcopy(mine, mine, lg_s.at[k], lg_r.at[zl], dev) for k, (_, dev) in enumerate(zpeers)]
    lc = [rcopy(mine, mine, lc_s.at[zl], lc_r.at[zl], sibling)]
    for copy in lg + lc:
        copy.start()
    for zz, _ in zpeers:
        ref = lt.at[zz // 2, zz % 2, c]
        rcopy(ref, ref, lg_s.at[0], lg_r.at[zz], sibling).wait_recv()
        copy = rcopy(ref, ref, lc_s.at[zz], lc_r.at[zz], sibling)
        copy.start()
        lc.append(copy)
    for zz in range(4):
        ref = lt.at[zz // 2, zz % 2, 1 - c]
        rcopy(ref, ref, lc_s.at[zz], lc_r.at[zz], sibling).wait_recv()

    p2 = rcopy(p_t.at[:, low, c], p_t.at[:, low, c], p2_s, p2_r, at(zh, x, y, zl + 1 - 2 * low, c))
    p2.start()
    pc = [rcopy(p_t.at[:, low, c], p_t.at[:, low, c], pc_s.at[0], pc_r.at[0], sibling)]
    pc[0].start()

    for t in range(2):
        for u in range(2):
            lt2[2 * t + u] = jnp.concatenate(
                [
                    lt[t, lo, cc, hi * 32 : hi * 32 + 32, u * 256 : u * 256 + 256]
                    for hi in range(2)
                    for lo in range(2)
                    for cc in range(2)
                ],
                axis=0,
            )

    own.wait()
    hs_in = hbuf.at[:, :, pl.ds(pl.multiple_of((1 - c) * 128, 128), 128)]
    rcopy(hs_in, hs_in, hs_s, hs_r, sibling).wait_recv()

    def project(distance):
        rnd, owner = OWNER[distance]
        block = (y + distance) % 8

        @pl.when(x != owner)
        def _():
            ref = hbuf.at[block, :, pl.ds(256, 768)]
            rcopy(ref, ref, hx_s.at[0, 0], hx_r.at[rnd, owner], sibling).wait_recv()

        total = jnp.zeros((224, 256), F32)
        for b in range(4):
            total = total + lax.dot_general(
                hbuf[block, :, b * 256 : b * 256 + 256], lt2[(zl + b) % 4],
                (((1,), (1,)), ((), ())), preferred_element_type=F32,
            )
        part[distance] = total

    def rs_copy(direction, h, step):
        rows = pl.ds(h * 112, 112)
        return rcopy(
            stage.at[direction, step, rows], arrived.at[direction, step, rows],
            rs_s.at[direction, h, step], rs_r.at[direction, h, step], up if direction == 0 else down,
        )

    rs = []

    def rs_send(direction, h, step):
        distance = 4 - step if direction == 0 else 4 + step
        rows = slice(h * 112, h * 112 + 112)
        value = part[distance, rows, :]
        begins = 0 if direction == h else 1
        if step > begins:
            rs_copy(direction, h, step - 1).wait_recv()
            value = value + arrived[direction, step - 1, rows, :].astype(F32)
        stage[direction, step, rows, :] = value.astype(BF)
        copy = rs_copy(direction, h, step)
        copy.start()
        rs.append(copy)

    project(4)
    rs_send(0, 0, 0)
    rs_send(1, 1, 0)
    project(3)
    rs_send(0, 1, 1)
    project(5)
    rs_send(1, 0, 1)
    rs_send(0, 0, 1)
    rs_send(1, 1, 1)
    project(2)
    project(6)
    for direction, h in ((0, 0), (1, 1), (0, 1), (1, 0)):
        rs_send(direction, h, 2)
    project(1)
    project(7)
    for direction, h in ((0, 0), (1, 1), (0, 1), (1, 0)):
        rs_send(direction, h, 3)
    project(0)

    dz, dx = [], []

    def gather_x(h, which, source):
        ref = dr.at[source, pl.ds(h * 112, 112)]
        for k, (_, dev) in enumerate(xpeers):
            copy = rcopy(ref, ref, dx_s.at[h, which, k], dx_r.at[h, source], dev)
            copy.start()
            dx.append(copy)

    for h in (0, 1):
        rows = slice(h * 112, h * 112 + 112)
        value = part[0, rows, :]
        for direction in (0, 1):
            rs_copy(direction, h, 3).wait_recv()
            value = value + arrived[direction, 3, rows, :].astype(F32)
        first_f = 0.9 * m1t[rows, :] + 0.1 * value
        second_f = 0.999 * m2t[rows, :] + 0.001 * value * value
        m1t[rows, :] = first_f
        m2t[rows, :] = second_f
        dr[rank, rows, :] = (first_f / FIRST_FIX / (jnp.sqrt(second_f / SECOND_FIX) + 1e-08)).astype(BF)
        ref = dr.at[rank, pl.ds(h * 112, 112)]
        copy = rcopy(ref, ref, dz_s.at[h], dz_r.at[h], partner)
        copy.start()
        dz.append(copy)
        gather_x(h, 0, rank)

    other = (1 - zh) * 4 + x
    for h in (0, 1):
        ref = dr.at[other, pl.ds(h * 112, 112)]
        rcopy(ref, ref, dz_s.at[h], dz_r.at[h], partner).wait_recv()
        gather_x(h, 1, other)

    ref = p_t.at[:, 1 - low, c]
    rcopy(ref, ref, p2_s, p2_r, sibling).wait_recv()
    pc.append(rcopy(ref, ref, pc_s.at[1], pc_r.at[1], sibling))
    pc[1].start()

    for src, dst in ((m1t, new1), (m2t, new2)):
        pad[...] = jnp.zeros_like(pad)
        pad[:224, :] = src[...]
        dst[...] = pad[...].T[:, :224].astype(BF)

    for k, lo in ((0, low), (1, 1 - low)):
        ref = p_t.at[:, lo, 1 - c]
        rcopy(ref, ref, pc_s.at[k], pc_r.at[k], sibling).wait_recv()
    for h in (0, 1):
        for half in (zh, 1 - zh):
            for sx, _ in xpeers:
                ref = dr.at[half * 4 + sx, pl.ds(h * 112, 112)]
                rcopy(ref, ref, dx_s.at[0, 0, 0], dx_r.at[h, half * 4 + sx], sibling).wait_recv()

    def columns(n, carry):
        lanes = pl.ds(pl.multiple_of(n * 256, 256), 256)
        total = jnp.zeros((224, 256), F32)
        for r in range(8):
            rows = jnp.concatenate(
                [
                    p_t[r, lo, cc, hi * 32 : hi * 32 + 32, lanes]
                    for hi in range(2)
                    for lo in range(2)
                    for cc in range(2)
                ],
                axis=0,
            )
            total = total + jnp.dot(dr[r], rows, preferred_element_type=F32)
        pad[:224, :] = total
        upd[lanes, :] = pad[...].T[:, :224].astype(BF)
        return carry

    lax.fori_loop(0, 4, columns, 0)

    pp.wait_send()
    for copy in ct + hz + hx + [hs, lz] + lg + lc + [p2] + pc + rs + dz + dx:
        copy.wait_send()
    for direction in (0, 1):
        for h in (0, 1):
            for step in range(4 if direction == h else 3):
                ring(direction, h, step).wait_send()
    for k in range(8):

        @pl.when(k % 4 != x)
        def _():
            left_copy(k).wait_send()


def per_device(cotangents, hidden, projector, moment_first, moment_second):
    dma = pltpu.SemaphoreType.DMA
    vmem = pl.BlockSpec(memory_space=pltpu.VMEM)
    return pl.pallas_call(
        body,
        out_shape=(
            jax.ShapeDtypeStruct((1024, 224), BF),
            jax.ShapeDtypeStruct((256, 224), BF),
            jax.ShapeDtypeStruct((256, 224), BF),
        ),
        in_specs=[vmem, pl.BlockSpec(memory_space=pl.ANY), vmem, vmem, vmem],
        out_specs=(vmem, vmem, vmem),
        scratch_shapes=[
            pltpu.VMEM((128, 14336), BF),
            pltpu.VMEM((8, 1792, 128), BF),
            pltpu.VMEM((8, 224, 1024), BF),
            pltpu.VMEM((8, 2, 2, 64, 1024), BF),
            pltpu.VMEM((1024, 512), BF),
            pltpu.VMEM((8, 64, 512), BF),
            pltpu.VMEM((4, 2, 64, 512), BF),
            pltpu.VMEM((64, 512), BF),
            pltpu.VMEM((64, 512), BF),
            pltpu.VMEM((2, 2, 2, 64, 512), BF),
            pltpu.VMEM((4, 256, 256), BF),
            pltpu.VMEM((8, 224, 256), F32),
            pltpu.VMEM((2, 4, 224, 256), BF),
            pltpu.VMEM((2, 4, 224, 256), BF),
            pltpu.VMEM((8, 224, 256), BF),
            pltpu.VMEM((224, 256), F32),
            pltpu.VMEM((224, 256), F32),
            pltpu.VMEM((256, 256), F32),
            dma((2,)),
            dma, dma,
            dma((3,)), dma((3,)),
            dma((2, 2, 4)), dma((2, 2, 4)),
            dma((2, 3, 2)), dma((2, 6)),
            dma((2, 3)), dma((2, 4)),
            dma, dma,
            dma((8,)), dma((4, 2)),
            dma, dma,
            dma((3,)), dma((4,)),
            dma((4,)), dma((4,)),
            dma, dma,
            dma((2,)), dma((2,)),
            dma((2, 2, 4)), dma((2, 2, 4)),
            dma((2,)), dma((2,)),
            dma((2, 2, 3)), dma((2, 8)),
        ],
        compiler_params=pltpu.CompilerParams(
            collective_id=0, has_side_effects=True, vmem_limit_bytes=48 * 2**20
        ),
        cost_estimate=pl.CostEstimate(flops=2_500_000_000, bytes_accessed=6_000_000, transcendentals=60_000),
        name="galore",
    )(cotangents, hidden, projector, moment_first, moment_second)


def solution(mesh):
    return jax.shard_map(
        per_device,
        mesh=mesh,
        in_specs=(
            P("fsdp", "rank"),
            P("fsdp", None),
            P("rank", "fsdp"),
            P("rank", "fsdp"),
            P("rank", "fsdp"),
        ),
        out_specs=(P("rank", "fsdp"), P("rank", "fsdp"), P("rank", "fsdp")),
        check_vma=False,
    )
```

```python
import jax
import jax.numpy as jnp
from jax import lax
from jax.experimental import pallas as pl
from jax.experimental.pallas import tpu as pltpu
from jax.sharding import PartitionSpec as P

STEP = 20
FIRST_FIX = 1.0 - 0.9**STEP
SECOND_FIX = 1.0 - 0.999**STEP
BF = jnp.bfloat16
F32 = jnp.float32
MESH = pl.DeviceIdType.MESH
OWNER = {4: (0, 0), 3: (0, 1), 5: (0, 2), 2: (0, 3), 0: (1, 0), 7: (1, 1), 1: (1, 2), 6: (1, 3)}
STOP = None
VL = 60
HID = True


def guarded(when, act):
    if when is None:
        act()
    else:
        pl.when(when)(act)


def kernel(*refs):
    state = {"in": {}, "out": [], "local": {}}
    for name in body(state, *refs):
        if name == STOP:
            break
    for copy in list(state["local"].values()):
        copy.wait()
    for copy, when in list(state["in"].values()):
        guarded(when, copy.wait_recv)
    for copy, when in state["out"]:
        guarded(when, copy.wait_send)


def body(
    state, cot, hid, prj, mom1, mom2,
    upd, new1, new2,
    hid_v, cot_v, hid_t, hbuf, p_t, cot_t, xs, xb, zs, zb, lt, part, stage, arrived, dr, m1, m2, n1, n2,
    loc_sem,
    pp_s, pp_r, ct_s, ct_r, ring_s, ring_r, hz_s, hz_r, hx_s, hx_r, hs_s, hs_r,
    ls_s, ls_r, lz_s, lz_r, lg_s, lg_r, lc_s, lc_r, p2_s, p2_r, pc_s, pc_r,
    rs_s, rs_r, dz_s, dz_r, dx_s, dx_r,
):
    inbox, outbox, local = state["in"], state["out"], state["local"]

    def send(copy, when=None):
        guarded(when, copy.start)
        outbox.append((copy, when))

    def expect(key, copy, when=None):
        inbox[key] = (copy, when)

    def receive(key):
        copy, when = inbox.pop(key)
        guarded(when, copy.wait_recv)

    def load(key, copy):
        copy.start()
        local[key] = copy

    def loaded(key):
        local.pop(key).wait()

    rank = lax.axis_index("rank")
    shard = lax.axis_index("fsdp")
    zh, x = rank // 4, rank % 4
    y, zl, c = shard // 8, (shard // 2) % 4, shard % 2
    z = zh * 4 + zl
    low, high = zl % 2, zl // 2

    def at(zh_, x_, y_, zl_, c_):
        return (zh_ * 4 + x_, y_ * 8 + zl_ * 2 + c_)

    def at_z(z_, c_):
        return at(z_ // 4, x, y, z_ % 4, c_)

    def at_y(step, other=False):
        return at(zh, x, (y + step + 8) % 8, (zl + 2) % 4 if other else zl, c)

    def rcopy(src, dst, ssem, rsem, dev):
        return pltpu.make_async_remote_copy(
            src_ref=src, dst_ref=dst, send_sem=ssem, recv_sem=rsem, device_id=dev, device_id_type=MESH
        )

    def landing(ref, sem):
        return rcopy(ref, ref, hs_s, sem, sibling)

    sibling = at(zh, x, y, zl, 1 - c)
    partner = at(1 - zh, x, y, zl, c)
    xpeers = [((x + k) % 4, at(zh, (x + k) % 4, y, zl, c)) for k in (1, 2, 3)]
    zpeers = [((zl + k) % 4, at(zh, x, y, (zl + k) % 4, c)) for k in (1, 2, 3)]

    def shard_ref(block, lo, hi):
        return p_t.at[block, c, lo, pl.ds(pl.multiple_of(hi * 32, 32), 32)]

    yield "start"
    load("prj", pltpu.make_async_copy(prj, shard_ref(y, low, high), loc_sem.at[0]))
    load("cot", pltpu.make_async_copy(cot, cot_v, loc_sem.at[1]))
    load("hid", pltpu.make_async_copy(hid, hid_v, loc_sem.at[2]))
    load("mom1", pltpu.make_async_copy(mom1, m1, loc_sem.at[3]))
    load("mom2", pltpu.make_async_copy(mom2, m2, loc_sem.at[4]))

    barrier = pltpu.get_barrier_semaphore()
    greet = [sibling, partner] + [d for _, d in xpeers] + [d for _, d in zpeers]
    greet += [at_y(1), at_y(-1), at_y(2), at_y(-2), at_y(1, True), at_y(-1, True)]
    greet += [at_z((z + off) % 8, cc) for off in (1, 7, 2, 6) for cc in (0, 1)]
    for dev in greet:
        pl.semaphore_signal(barrier, inc=1, device_id=dev, device_id_type=MESH)

    def cot_ref(lo, cc):
        return cot_t.at[:, pl.ds(pl.multiple_of(lo * 256 + cc * 128, 128), 128)]

    loaded("cot")
    cot_t[:, pl.ds(pl.multiple_of(low * 256 + c * 128, 128), 128)] = cot_v[...].T
    loaded("prj")
    yield "barrier"
    pl.semaphore_wait(barrier, len(greet))
    yield "first_sends"

    def ring_ref(block, kind):
        return shard_ref(block, low, high if kind == 0 else 1 - high)

    def ring_send(direction, kind, step):
        sign = 1 - 2 * direction
        sems = ring_s.at[direction, kind, step], ring_r.at[direction, kind, step]
        origin = (y - sign * min(step, 2) + 8) % 8
        ref = ring_ref(origin, kind)
        send(rcopy(ref, ref, *sems, at_y(sign * (2 if step == 3 else 1))))

    def ring_expect(direction, kind, step):
        origin = (y - (1 - 2 * direction) * (step + 1) + 8) % 8
        expect(("ring", direction, kind, step), landing(ring_ref(origin, kind), ring_r.at[direction, kind, step]))

    own_shard = ring_ref(y, 0)
    for direction in (0, 1):
        sign = 1 - 2 * direction
        for kind in (0, 1):
            send(rcopy(own_shard, own_shard, ring_s.at[direction, kind, 0], ring_r.at[direction, kind, 0],
                       at_y(sign, kind == 1)))
            ring_expect(direction, kind, 0)

    def shard_send(k):
        zz, dev = zpeers[k - 1]
        send(rcopy(own_shard, own_shard, pp_s.at[k], pp_r.at[k], dev))
        source = (zl + 4 - k) % 4
        expect(("pp", k), landing(shard_ref(y, source % 2, source // 2), pp_r.at[k]))

    shard_send(2)

    def cot_send(ref, k, dev):
        send(rcopy(ref, ref, ct_s.at[k], ct_r.at[k], dev))

    cot_send(cot_ref(low, c), 0, at(zh, x, y, zl + 1 - 2 * low, c))
    cot_send(cot_ref(low, c), 1, sibling)
    expect("cot0", landing(cot_ref(1 - low, c), ct_r.at[0]))
    expect("cot1", landing(cot_ref(low, 1 - c), ct_r.at[1]))

    def transpose_block(block):
        def tile(t, carry):
            column = pl.multiple_of(block * 1792 + t * 128, 128)
            row = pl.multiple_of(t * 128, 128)
            hid_t[block, pl.ds(row, 128), :] = hid_v[:, pl.ds(column, 128)].T
            return carry

        lax.fori_loop(0, 14, tile, 0, unroll=7)

    first = jnp.where(x == 0, 4, jnp.where(x == 1, 3, jnp.where(x == 2, 5, 2)))
    blocks = [(y + first) % 8, (y + first + 4) % 8]

    def hidden_send(rnd):
        if not HID:
            return
        block = blocks[rnd]
        for k, (off, rot) in enumerate(((1, 3), (7, 1), (None, 2))):
            zd = (z + off) % 8 if off is not None else (z + 2 + 4 * c) % 8
            lane = pl.multiple_of(rot * 256 + c * 128, 128)
            for cc in (0, 1):
                row = pl.multiple_of((2 * (zd % 4) + cc) * 224, 16)
                send(rcopy(
                    hid_t.at[block, pl.ds(row, 224)], hbuf.at[block, :, pl.ds(lane, 128)],
                    hz_s.at[rnd, k, cc], hz_r.at[rnd, 2 * k + c], at_z(zd, cc),
                ))
                ref = hbuf.at[block, :, pl.ds(rot * 256 + cc * 128, 128)]
                expect(("hz", rnd, k, cc), landing(ref, hz_r.at[rnd, 2 * k + cc]))

    def hidden_forward(rnd):
        if not HID:
            return
        for k in range(3):
            for cc in (0, 1):
                receive(("hz", rnd, k, cc))
        ref = hbuf.at[blocks[rnd], :, pl.ds(256, 768)]
        for k, (_, dev) in enumerate(xpeers):
            send(rcopy(ref, ref, hx_s.at[rnd, k], hx_r.at[rnd, x], dev))
        for distance, (when, owner) in OWNER.items():
            if when == rnd:
                ref = hbuf.at[(y + distance) % 8, :, pl.ds(256, 768)]
                expect(("hx", distance), landing(ref, hx_r.at[rnd, owner]), x != owner)

    yield "hidden_sends"
    loaded("hid")
    for rnd in (0, 1):
        transpose_block(blocks[rnd])
        hidden_send(rnd)
    shard_send(1)
    shard_send(3)

    yield "ring_0"
    for kind in (0, 1):
        for direction in (0, 1):
            receive(("ring", direction, kind, 0))
            ring_send(direction, kind, 1)
            ring_expect(direction, kind, 1)
    for k in range(1, 4):
        transpose_block((blocks[0] + k) % 8)

    yield "ring_1"
    for kind in (0, 1):
        for direction in (0, 1):
            receive(("ring", direction, kind, 1))
            ring_send(direction, kind, 2)
            ring_expect(direction, kind, 2)
            if kind == direction:
                ring_send(direction, kind, 3)
                ring_expect(direction, kind, 3)

    yield "cot_wait"
    receive("cot0")
    cot_send(cot_ref(1 - low, c), 2, sibling)
    expect("cot2", landing(cot_ref(1 - low, 1 - c), ct_r.at[2]))
    for k in range(5, 8):
        transpose_block((blocks[0] + k) % 8)
    hs_lane = pl.ds(pl.multiple_of(c * 128, 128), 128)
    load("own", pltpu.make_async_copy(
        hid_t.at[:, pl.ds(pl.multiple_of((2 * zl + c) * 224, 16), 224)], hbuf.at[:, :, hs_lane], loc_sem.at[5]
    ))
    send(rcopy(
        hid_t.at[:, pl.ds(pl.multiple_of((2 * zl + 1 - c) * 224, 16), 224)], hbuf.at[:, :, hs_lane], hs_s, hs_r, sibling
    ))
    expect("hs", landing(hbuf.at[:, :, pl.ds(pl.multiple_of((1 - c) * 128, 128), 128)], hs_r))
    receive("cot1")
    receive("cot2")
    receive(("pp", 2))

    def left_block(block):
        rows = p_t[block, c, low]
        xs[block] = jnp.dot(rows, cot_t[...], preferred_element_type=F32).astype(BF)
        send(rcopy(
            xs.at[block], xb.at[x, block // 4], ls_s.at[block], ls_r.at[x, block // 4], at(zh, block % 4, y, zl, c)
        ), block % 4 != x)

    yield "left_first"
    for distance in (0, 1, 7, 2, 6):
        left_block((y + distance) % 8)

    yield "ring_2"
    for kind in (0, 1):
        for direction in (0, 1):
            receive(("ring", direction, kind, 2))
    left_block((y + 3) % 8)
    left_block((y + 5) % 8)
    yield "ring_3"
    receive(("ring", 0, 0, 3))
    receive(("ring", 1, 1, 3))
    left_block((y + 4) % 8)

    def rest_send(direction, step):
        sign = 1 - 2 * direction
        origin = (y - sign * min(step, 2) + 8) % 8
        ref = p_t.at[origin, c, 1 - low] if step < 3 else shard_ref(origin, 1 - low, direction)
        send(rcopy(ref, ref, p2_s.at[direction, step], p2_r.at[direction, step], at_y(sign * (2 if step == 3 else 1))))
        origin = (y - sign * (step + 1) + 8) % 8
        ref = p_t.at[origin, c, 1 - low] if step < 3 else shard_ref(origin, 1 - low, direction)
        expect(("p2", direction, step), landing(ref, p2_r.at[direction, step]))

    yield "hidden_forward_0"
    hidden_forward(0)
    yield "rest_0"
    receive(("pp", 1))
    receive(("pp", 3))
    for direction in (0, 1):
        rest_send(direction, 0)

    def left_wait(side):
        for k in range(3):
            receive(("ls", k, side))

    def left_sum(half):
        total = xs[half * 4 + x].astype(F32)
        for sx, _ in xpeers:
            total = total + xb[sx, half].astype(F32)
        return total

    for k, (sx, _) in enumerate(xpeers):
        for side, half in enumerate((zh, 1 - zh)):
            expect(("ls", k, side), landing(xb.at[sx, half], ls_r.at[sx, half]))

    yield "left_x_wait"
    left_wait(1)
    zs[...] = left_sum(1 - zh).astype(BF)
    send(rcopy(zs, zb, lz_s, lz_r, partner))
    expect("lz", landing(zb, lz_r))
    yield "rest_1"
    for direction in (0, 1):
        receive(("p2", direction, 0))
        rest_send(direction, 1)
    left_wait(0)
    yield "left_z_wait"
    receive("lz")
    mine = lt.at[high, c, low]
    lt[high, c, low] = (left_sum(zh) + zb[...].astype(F32)).astype(BF)
    for k, (zz, dev) in enumerate(zpeers):
        send(rcopy(mine, mine, lg_s.at[k], lg_r.at[zl], dev))
        expect(("lg", k), landing(lt.at[zz // 2, c, zz % 2], lg_r.at[zz]))
    send(rcopy(mine, mine, lc_s.at[zl], lc_r.at[zl], sibling))
    for zz in range(4):
        expect(("lc", zz), landing(lt.at[zz // 2, 1 - c, zz % 2], lc_r.at[zz]))
    yield "hidden_forward_1"
    hidden_forward(1)
    yield "rest_2"
    for direction in (0, 1):
        receive(("p2", direction, 1))
        rest_send(direction, 2)
        rest_send(direction, 3)
    yield "left_gather"
    for k, (zz, _) in enumerate(zpeers):
        receive(("lg", k))
        ref = lt.at[zz // 2, c, zz % 2]
        send(rcopy(ref, ref, lc_s.at[zz], lc_r.at[zz], sibling))

    yield "hidden_local"
    loaded("own")
    receive("hs")

    def project(distance, half):
        block = (y + distance) % 8
        if half == 0 and HID:
            receive(("hx", distance))
        cc = c if half == 0 else 1 - c
        total = jnp.zeros((224, 128), F32)
        for b in range(4):
            zz = (zl + b) % 4
            weights = lt[zz // 2, cc, :, :, pl.ds(pl.multiple_of((zz % 2) * 256, 256), 256)].reshape(128, 256)
            total = total + lax.dot_general(
                hbuf[block, :, b * 256 : b * 256 + 256], weights,
                (((1,), (1,)), ((), ())), preferred_element_type=F32,
            )
        part[distance, half] = total

    def sum_copy(direction, half, step):
        sign = 1 - 2 * direction
        return rcopy(
            stage.at[direction, half, step], arrived.at[direction, half, step],
            rs_s.at[direction, half, step], rs_r.at[direction, half, step], at_y(sign * (2 if step == 0 else 1)),
        )

    def sum_send(direction, half, step):
        distance = 4 - step if direction == 0 else 4 + step
        value = part[distance, half]
        sources = [1] + ([0] if half == direction else []) if step == 2 else [2] if step == 3 else []
        for source in sources:
            receive(("sum", direction, half, source))
            value = value + arrived[direction, half, source].astype(F32)
        stage[direction, half, step] = value.astype(BF)
        copy = sum_copy(direction, half, step)
        send(copy)
        expect(("sum", direction, half, step), copy)

    yield "sum_0"
    for half in (0, 1):
        if half == 1:
            for zz in range(4):
                receive(("lc", zz))
        project(4, half)
        sum_send(half, half, 0)
        project(3, half)
        sum_send(0, half, 1)
        project(5, half)
        sum_send(1, half, 1)
    yield "sum_1"
    for half in (0, 1):
        project(2, half)
        project(6, half)
        sum_send(0, half, 2)
        sum_send(1, half, 2)
    yield "rest_3"
    for direction in (0, 1):
        receive(("p2", direction, 2))
        receive(("p2", direction, 3))
    send(rcopy(p_t.at[:, c], p_t.at[:, c], pc_s, pc_r, sibling))
    expect("pc", landing(p_t.at[:, 1 - c], pc_r))
    yield "sum_2"
    for half in (0, 1):
        project(1, half)
        project(7, half)
        sum_send(0, half, 3)
        sum_send(1, half, 3)
    for half in (0, 1):
        project(0, half)

    row = lax.broadcasted_iota(jnp.int32, (256, 256), 0)
    column = lax.broadcasted_iota(jnp.int32, (256, 256), 1)
    swapped = (row // 128) * 32 + ((row // 64) % 2) * 64 + ((row // 32) % 2) * 128 + row % 32
    order = jnp.where(swapped == column, 1.0, 0.0).astype(BF)
    loaded("mom1")
    loaded("mom2")
    n1[...] = jnp.dot(m1[...], order, preferred_element_type=F32)
    n2[...] = jnp.dot(m2[...], order, preferred_element_type=F32)

    def gather_x(half, which, source, lanes):
        ref = dr.at[source, :, lanes]
        for k, (sx, dev) in enumerate(xpeers):
            send(rcopy(ref, ref, dx_s.at[half, which, k], dx_r.at[half, source], dev))
            peer = source - x + sx
            expect(("dx", half, which, k), landing(dr.at[peer, :, lanes], dx_r.at[half, peer]))

    other = (1 - zh) * 4 + x
    lane_sets = []
    for half in (0, 1):
        yield "sum_end_%d" % half
        value = part[0, half]
        for direction in (0, 1):
            receive(("sum", direction, half, 3))
            value = value + arrived[direction, half, 3].astype(F32)
        lanes = pl.ds(pl.multiple_of((c if half == 0 else 1 - c) * 128, 128), 128)
        lane_sets.append(lanes)
        first_f = 0.9 * n1[:, lanes] + 0.1 * value
        second_f = 0.999 * n2[:, lanes] + 0.001 * value * value
        dr[rank, :, lanes] = (first_f / FIRST_FIX / (jnp.sqrt(second_f / SECOND_FIX) + 1e-08)).astype(BF)
        send(rcopy(dr.at[rank, :, lanes], dr.at[rank, :, lanes], dz_s.at[half], dz_r.at[half], partner))
        expect(("dz", half), landing(dr.at[other, :, lanes], dz_r.at[half]))
        gather_x(half, 0, rank, lanes)
        n1[:, lanes] = first_f
        n2[:, lanes] = second_f

    new1[...] = jnp.dot(n1[...].astype(BF), order, preferred_element_type=F32).astype(BF)
    new2[...] = jnp.dot(n2[...].astype(BF), order, preferred_element_type=F32).astype(BF)
    yield "dir_z_wait"
    for half in (0, 1):
        receive(("dz", half))
        gather_x(half, 1, other, lane_sets[half])
    yield "proj_core_wait"
    receive("pc")
    yield "dir_x_wait"
    for which in (0, 1):
        for half in (0, 1):
            for k in range(3):
                receive(("dx", half, which, k))

    yield "update"

    def columns(n, carry):
        lanes = pl.ds(pl.multiple_of(n * 256, 256), 256)
        total = jnp.zeros((224, 256), F32)
        for r in range(8):
            rows = p_t[r, :, :, :, lanes].reshape(256, 256)
            total = total + jnp.dot(dr[r], rows, preferred_element_type=F32)
        upd[:, lanes] = total.astype(BF)
        return carry

    lax.fori_loop(0, 4, columns, 0)


def hand_over(*refs):
    for k in range(3):
        refs[3 + k][...] = refs[k][...]


def per_device(cotangents, hidden, projector, moment_first, moment_second):
    dma = pltpu.SemaphoreType.DMA
    vmem = pl.BlockSpec(memory_space=pltpu.VMEM)
    anywhere = pl.BlockSpec(memory_space=pl.ANY)
    shapes = (
        jax.ShapeDtypeStruct((224, 1024), BF),
        jax.ShapeDtypeStruct((224, 256), BF),
        jax.ShapeDtypeStruct((224, 256), BF),
    )
    results = pl.pallas_call(
        kernel,
        out_shape=shapes,
        in_specs=[pl.BlockSpec(memory_space=pl.ANY)] * 5,
        out_specs=(vmem, vmem, vmem),
        scratch_shapes=[
            pltpu.VMEM((128, 14336), BF),
            pltpu.VMEM((128, 1024), BF),
            pltpu.VMEM((8, 1792, 128), BF),
            pltpu.VMEM((8, 224, 1024), BF),
            pltpu.VMEM((8, 2, 2, 64, 1024), BF),
            pltpu.VMEM((1024, 512), BF),
            pltpu.VMEM((8, 64, 512), BF),
            pltpu.VMEM((4, 2, 64, 512), BF),
            pltpu.VMEM((64, 512), BF),
            pltpu.VMEM((64, 512), BF),
            pltpu.VMEM((2, 2, 2, 64, 512), BF),
            pltpu.VMEM((8, 2, 224, 128), F32),
            pltpu.VMEM((2, 2, 4, 224, 128), BF),
            pltpu.VMEM((2, 2, 4, 224, 128), BF),
            pltpu.VMEM((8, 224, 256), BF),
            pltpu.VMEM((224, 256), BF),
            pltpu.VMEM((224, 256), BF),
            pltpu.VMEM((224, 256), F32),
            pltpu.VMEM((224, 256), F32),
            dma((6,)),
            dma((4,)), dma((4,)),
            dma((3,)), dma((3,)),
            dma((2, 2, 4)), dma((2, 2, 4)),
            dma((2, 3, 2)), dma((2, 6)),
            dma((2, 3)), dma((2, 4)),
            dma, dma,
            dma((8,)), dma((4, 2)),
            dma, dma,
            dma((3,)), dma((4,)),
            dma((4,)), dma((4,)),
            dma((2, 4)), dma((2, 4)),
            dma, dma,
            dma((2, 2, 4)), dma((2, 2, 4)),
            dma((2,)), dma((2,)),
            dma((2, 2, 3)), dma((2, 8)),
        ],
        compiler_params=pltpu.CompilerParams(
            collective_id=0, has_side_effects=True, vmem_limit_bytes=VL * 2**20
        ),
        cost_estimate=pl.CostEstimate(flops=2_500_000_000, bytes_accessed=6_000_000, transcendentals=60_000),
        name="galore",
    )(cotangents, hidden, projector.T, moment_first.T, moment_second.T)
    results = pl.pallas_call(
        hand_over,
        out_shape=shapes,
        in_specs=[vmem] * 3,
        out_specs=(vmem,) * 3,
        cost_estimate=pl.CostEstimate(flops=0, bytes_accessed=1_400_000, transcendentals=0),
        name="hand_over",
    )(*results)
    return tuple(array.T for array in results)


def solution(mesh):
    return jax.shard_map(
        per_device,
        mesh=mesh,
        in_specs=(
            P("fsdp", "rank"),
            P("fsdp", None),
            P("rank", "fsdp"),
            P("rank", "fsdp"),
            P("rank", "fsdp"),
        ),
        out_specs=(P("rank", "fsdp"), P("rank", "fsdp"), P("rank", "fsdp")),
        check_vma=False,
    )
```

```python
import jax
import jax.numpy as jnp
from jax import lax
from jax.experimental import pallas as pl
from jax.experimental.pallas import tpu as pltpu
from jax.sharding import PartitionSpec as P

STEP = 20
FIRST_FIX = 1.0 - 0.9**STEP
SECOND_FIX = 1.0 - 0.999**STEP
BF = jnp.bfloat16
F32 = jnp.float32
MESH = pl.DeviceIdType.MESH
STOP = None
VL = 60
HID = True


def guarded(when, act):
    if when is None:
        act()
    else:
        pl.when(when)(act)


def kernel(*refs):
    state = {"in": {}, "out": [], "local": {}}
    for name in body(state, *refs):
        if name == STOP:
            break
    for copy in list(state["local"].values()):
        copy.wait()
    for copy, when in list(state["in"].values()):
        guarded(when, copy.wait_recv)
    for copy, when in state["out"]:
        guarded(when, copy.wait_send)


def body(
    state, cot, hid, prj, mom1, mom2,
    upd, new1, new2,
    hid_v, cot_v, hid_t, hbuf, p_t, cot_t, xs, xb, zs, zb, lt, part, stage, arrived, dr, m1, m2, n1, n2, acc, upd_v,
    loc_sem, out_sem,
    pp_s, pp_r, ct_s, ct_r, ring_s, ring_r, hz_s, hz_r, hx_s, hx_r, hs_s, hs_r,
    ls_s, ls_r, lz_s, lz_r, lg_s, lg_r, lc_s, lc_r, p2_s, p2_r, pc_s, pc_r,
    rs_s, rs_r, dz_s, dz_r, dx_s, dx_r,
):
    inbox, outbox, local = state["in"], state["out"], state["local"]

    def send(copy, when=None):
        guarded(when, copy.start)
        outbox.append((copy, when))

    def expect(key, copy, when=None):
        inbox[key] = (copy, when)

    def receive(key):
        copy, when = inbox.pop(key)
        guarded(when, copy.wait_recv)

    def load(key, copy):
        copy.start()
        local[key] = copy

    def loaded(key):
        local.pop(key).wait()

    rank = lax.axis_index("rank")
    shard = lax.axis_index("fsdp")
    zh, x = rank // 4, rank % 4
    y, zl, c = shard // 8, (shard // 2) % 4, shard % 2
    z = zh * 4 + zl
    low, high = zl % 2, zl // 2

    def at(zh_, x_, y_, zl_, c_):
        return (zh_ * 4 + x_, y_ * 8 + zl_ * 2 + c_)

    def at_z(z_, c_):
        return at(z_ // 4, x, y, z_ % 4, c_)

    def at_y(step):
        return at(zh, x, (y + step + 8) % 8, zl, c)

    def rcopy(src, dst, ssem, rsem, dev):
        return pltpu.make_async_remote_copy(
            src_ref=src, dst_ref=dst, send_sem=ssem, recv_sem=rsem, device_id=dev, device_id_type=MESH
        )

    def landing(ref, sem):
        return rcopy(ref, ref, hs_s, sem, sibling)

    sibling = at(zh, x, y, zl, 1 - c)
    partner = at(1 - zh, x, y, zl, c)
    xpeers = [((x + k) % 4, at(zh, (x + k) % 4, y, zl, c)) for k in (1, 2, 3)]
    zpeers = [((zl + k) % 4, at(zh, x, y, (zl + k) % 4, c)) for k in (1, 2, 3)]

    def shard_ref(block, lo, hi):
        return p_t.at[block, c, lo, pl.ds(pl.multiple_of(hi * 32, 32), 32)]

    yield "start"
    load("prj", pltpu.make_async_copy(prj, shard_ref(y, low, high), loc_sem.at[0]))
    load("cot", pltpu.make_async_copy(cot, cot_v, loc_sem.at[1]))
    load("hid", pltpu.make_async_copy(hid, hid_v, loc_sem.at[2]))
    load("mom1", pltpu.make_async_copy(mom1, m1, loc_sem.at[3]))
    load("mom2", pltpu.make_async_copy(mom2, m2, loc_sem.at[4]))

    barrier = pltpu.get_barrier_semaphore()
    greet = [sibling, partner] + [d for _, d in xpeers] + [d for _, d in zpeers]
    greet += [at_y(1), at_y(-1), at_y(2), at_y(-2)]
    greet += [at_z((z + off) % 8, cc) for off in (1, 7, 2, 6) for cc in (0, 1)]
    for dev in greet:
        pl.semaphore_signal(barrier, inc=1, device_id=dev, device_id_type=MESH)

    def cot_ref(lo, cc):
        return cot_t.at[:, pl.ds(pl.multiple_of(lo * 256 + cc * 128, 128), 128)]

    loaded("cot")
    cot_t[:, pl.ds(pl.multiple_of(low * 256 + c * 128, 128), 128)] = cot_v[...].T
    loaded("prj")
    yield "barrier"
    pl.semaphore_wait(barrier, len(greet))
    yield "first_sends"

    def ring_ref(block, kind):
        return shard_ref(block, low, high if kind == 0 else 1 - high)

    def ring_send(direction, kind, step):
        sign = 1 - 2 * direction
        sems = ring_s.at[direction, kind, step], ring_r.at[direction, kind, step]
        origin = (y - sign * min(step, 2) + 8) % 8
        ref = ring_ref(origin, kind)
        send(rcopy(ref, ref, *sems, at_y(sign * (2 if step == 3 else 1))))

    def ring_expect(direction, kind, step):
        origin = (y - (1 - 2 * direction) * (step + 1) + 8) % 8
        expect(("ring", direction, kind, step), landing(ring_ref(origin, kind), ring_r.at[direction, kind, step]))

    own_shard = ring_ref(y, 0)

    def shard_send(k):
        zz, dev = zpeers[k - 1]
        send(rcopy(own_shard, own_shard, pp_s.at[k], pp_r.at[k], dev))
        source = (zl + 4 - k) % 4
        expect(("pp", k), landing(shard_ref(y, source % 2, source // 2), pp_r.at[k]))

    shard_send(2)
    for direction in (0, 1):
        ring_send(direction, 0, 0)
        for kind in (0, 1):
            ring_expect(direction, kind, 0)

    def cot_send(ref, k, dev):
        send(rcopy(ref, ref, ct_s.at[k], ct_r.at[k], dev))

    cot_send(cot_ref(low, c), 1, sibling)
    expect("cot1", landing(cot_ref(low, 1 - c), ct_r.at[1]))

    def transpose_block(block):
        def tile(t, carry):
            column = pl.multiple_of(block * 1792 + t * 128, 128)
            row = pl.multiple_of(t * 128, 128)
            hid_t[block, pl.ds(row, 128), :] = hid_v[:, pl.ds(column, 128)].T
            return carry

        lax.fori_loop(0, 14, tile, 0, unroll=7)

    def fetched(position, rnd):
        first = jnp.where(position == 0, 4, jnp.where(position == 1, 3, jnp.where(position == 2, 5, 2)))
        return (y + first + 4 * rnd) % 8

    blocks = [fetched(x, rnd) for rnd in (0, 1)]

    def hidden_send(rnd):
        if not HID:
            return
        block = blocks[rnd]
        for k, (off, rot) in enumerate(((1, 3), (7, 1), (None, 2))):
            zd = (z + off) % 8 if off is not None else (z + 2 + 4 * c) % 8
            lane = pl.multiple_of(rot * 256 + c * 128, 128)
            for cc in (0, 1):
                row = pl.multiple_of((2 * (zd % 4) + cc) * 224, 16)
                send(rcopy(
                    hid_t.at[block, pl.ds(row, 224)], hbuf.at[block, :, pl.ds(lane, 128)],
                    hz_s.at[rnd, k, cc], hz_r.at[rnd, 2 * k + c], at_z(zd, cc),
                ))
                ref = hbuf.at[block, :, pl.ds(rot * 256 + cc * 128, 128)]
                expect(("hz", rnd, k, cc), landing(ref, hz_r.at[rnd, 2 * k + cc]))

    def hidden_forward(rnd):
        if not HID:
            return
        for k in range(3):
            for cc in (0, 1):
                receive(("hz", rnd, k, cc))
        ref = hbuf.at[blocks[rnd], :, pl.ds(256, 768)]
        for side in (0, 1):
            send(rcopy(ref, ref, hx_s.at[rnd, side], hx_r.at[rnd, side], xpeers[2 * side][1]))
            near = fetched((x + 3 + 2 * side) % 4, rnd)
            expect(("hx", rnd, side), landing(hbuf.at[near, :, pl.ds(256, 768)], hx_r.at[rnd, side]))

    def hidden_further(rnd):
        if not HID:
            return
        far = fetched((x + 2) % 4, rnd)
        for side in (0, 1):
            receive(("hx", rnd, side))
            near = fetched((x + 3 + 2 * side) % 4, rnd)
            rows = pl.ds(side * 112, 112)
            ref = hbuf.at[near, rows, pl.ds(256, 768)]
            send(rcopy(ref, ref, hx_s.at[rnd, 2 + side], hx_r.at[rnd, 2 + side], xpeers[2 * side][1]))
            expect(("hx", rnd, 2 + side), landing(hbuf.at[far, rows, pl.ds(256, 768)], hx_r.at[rnd, 2 + side]))

    def hidden_wait(rnd):
        if not HID:
            return
        for side in (0, 1):
            receive(("hx", rnd, 2 + side))

    def ring_pass(direction, kind, step):
        receive(("ring", direction, kind, step))
        ring_send(direction, kind, step + 1)
        ring_expect(direction, kind, step + 1)
        if step == 1 and kind == direction:
            ring_send(direction, kind, 3)
            ring_expect(direction, kind, 3)

    yield "hidden_sends"
    loaded("hid")
    transpose_block(blocks[0])
    hidden_send(0)
    transpose_block(blocks[1])
    yield "pair"
    cot_send(cot_ref(low, c), 0, at(zh, x, y, zl + 1 - 2 * low, c))
    expect("cot0", landing(cot_ref(1 - low, c), ct_r.at[0]))
    receive(("pp", 2))
    for direction in (0, 1):
        ring_send(direction, 1, 0)
    yield "ring_0"
    ring_pass(0, 0, 0)
    ring_pass(1, 0, 0)
    for k in range(1, 4):
        transpose_block((blocks[0] + k) % 8)
    yield "ring_0_1"
    ring_pass(0, 1, 0)
    ring_pass(1, 1, 0)
    ring_pass(0, 0, 1)
    ring_pass(1, 0, 1)
    hidden_send(1)
    for k in range(5, 8):
        transpose_block((blocks[0] + k) % 8)
    yield "hidden_forward_0"
    hidden_forward(0)
    yield "ring_1_1"
    ring_pass(0, 1, 1)
    ring_pass(1, 1, 1)

    hs_lane = pl.ds(pl.multiple_of(c * 128, 128), 128)
    load("own", pltpu.make_async_copy(
        hid_t.at[:, pl.ds(pl.multiple_of((2 * zl + c) * 224, 16), 224)], hbuf.at[:, :, hs_lane], loc_sem.at[5]
    ))
    send(rcopy(
        hid_t.at[:, pl.ds(pl.multiple_of((2 * zl + 1 - c) * 224, 16), 224)], hbuf.at[:, :, hs_lane], hs_s, hs_r, sibling
    ))
    expect("hs", landing(hbuf.at[:, :, pl.ds(pl.multiple_of((1 - c) * 128, 128), 128)], hs_r))
    yield "cot_wait"
    receive("cot0")
    cot_send(cot_ref(1 - low, c), 2, sibling)
    expect("cot2", landing(cot_ref(1 - low, 1 - c), ct_r.at[2]))
    receive("cot1")
    receive("cot2")
    shard_send(1)
    shard_send(3)

    def left_block(block):
        rows = p_t[block, c, low]
        xs[block] = jnp.dot(rows, cot_t[...], preferred_element_type=F32).astype(BF)
        send(rcopy(
            xs.at[block], xb.at[x, block // 4], ls_s.at[block], ls_r.at[x, block // 4], at(zh, block % 4, y, zl, c)
        ), block % 4 != x)

    yield "left_first"
    for distance in (0, 1, 7, 2, 6):
        left_block((y + distance) % 8)

    yield "ring_2"
    for kind in (0, 1):
        for direction in (0, 1):
            receive(("ring", direction, kind, 2))
    left_block((y + 3) % 8)
    left_block((y + 5) % 8)
    yield "ring_3"
    receive(("ring", 0, 0, 3))
    receive(("ring", 1, 1, 3))
    left_block((y + 4) % 8)

    def rest_send_y():
        for direction in (0, 1):
            sign = 1 - 2 * direction
            ref = p_t.at[y, c, 1 - low]
            send(rcopy(ref, ref, p2_s.at[direction], p2_r.at[direction], at_y(sign)))
            expect(("p2", direction), landing(p_t.at[(y - sign + 8) % 8, c, 1 - low], p2_r.at[direction]))

    def core_send(k):
        lo = low if k == 0 else 1 - low
        ref = p_t.at[:, c, lo]
        send(rcopy(ref, ref, pc_s.at[k], pc_r.at[k], sibling))
        expect(("pc", k), landing(p_t.at[:, 1 - c, lo], pc_r.at[k]))

    def rest_send_z():
        for k in range(2, 7):
            ref = p_t.at[(y + k) % 8, c, low]
            send(rcopy(ref, ref, p2_s.at[k], p2_r.at[k], at(zh, x, y, zl + 1 - 2 * low, c)))
            expect(("p2", k), landing(p_t.at[(y + k) % 8, c, 1 - low], p2_r.at[k]))

    yield "hidden_further_0"
    hidden_further(0)
    yield "hidden_forward_1"
    hidden_forward(1)

    def left_wait(side):
        for k in range(3):
            receive(("ls", k, side))

    def left_sum(half):
        total = xs[half * 4 + x].astype(F32)
        for sx, _ in xpeers:
            total = total + xb[sx, half].astype(F32)
        return total

    for k, (sx, _) in enumerate(xpeers):
        for side, half in enumerate((zh, 1 - zh)):
            expect(("ls", k, side), landing(xb.at[sx, half], ls_r.at[sx, half]))

    yield "left_x_wait"
    left_wait(1)
    zs[...] = left_sum(1 - zh).astype(BF)
    send(rcopy(zs, zb, lz_s, lz_r, partner))
    expect("lz", landing(zb, lz_r))
    yield "rest_0"
    receive(("pp", 1))
    receive(("pp", 3))
    rest_send_y()
    left_wait(0)
    yield "left_z_wait"
    receive("lz")
    mine = lt.at[high, c, low]
    lt[high, c, low] = (left_sum(zh) + zb[...].astype(F32)).astype(BF)
    for k, (zz, dev) in enumerate(zpeers):
        send(rcopy(mine, mine, lg_s.at[k], lg_r.at[zl], dev))
        expect(("lg", k), landing(lt.at[zz // 2, c, zz % 2], lg_r.at[zz]))
    send(rcopy(mine, mine, lc_s.at[zl], lc_r.at[zl], sibling))
    expect(("lc", 0), landing(lt.at[high, 1 - c, low], lc_r.at[zl]))
    yield "hidden_further_1"
    hidden_further(1)
    yield "left_gather"
    for k, (zz, _) in enumerate(zpeers):
        receive(("lg", k))
        ref = lt.at[zz // 2, c, zz % 2]
        send(rcopy(ref, ref, lc_s.at[zz], lc_r.at[zz], sibling))
        expect(("lc", k + 1), landing(lt.at[zz // 2, 1 - c, zz % 2], lc_r.at[zz]))

    rest_send_z()
    core_send(0)
    yield "hidden_local"
    loaded("own")
    receive("hs")

    def project(distance, half):
        block = (y + distance) % 8
        cc = c if half == 0 else 1 - c
        total = jnp.zeros((224, 128), F32)
        for b in range(4):
            zz = (zl + b) % 4
            weights = lt[zz // 2, cc, :, :, pl.ds(pl.multiple_of((zz % 2) * 256, 256), 256)].reshape(128, 256)
            total = total + lax.dot_general(
                hbuf[block, :, b * 256 : b * 256 + 256], weights,
                (((1,), (1,)), ((), ())), preferred_element_type=F32,
            )
        part[distance, half] = total

    def sum_copy(direction, half, step):
        sign = 1 - 2 * direction
        return rcopy(
            stage.at[direction, half, step], arrived.at[direction, half, step],
            rs_s.at[direction, half, step], rs_r.at[direction, half, step], at_y(sign * (2 if step == 0 else 1)),
        )

    def sum_send(direction, half, step):
        distance = 4 - step if direction == 0 else 4 + step
        value = part[distance, half]
        sources = [1] + ([0] if half == direction else []) if step == 2 else [2] if step == 3 else []
        for source in sources:
            receive(("sum", direction, half, source))
            value = value + arrived[direction, half, source].astype(F32)
        stage[direction, half, step] = value.astype(BF)
        copy = sum_copy(direction, half, step)
        send(copy)
        expect(("sum", direction, half, step), copy)

    yield "hidden_wait_0"
    hidden_wait(0)
    yield "sum_0"
    for half in (0, 1):
        if half == 1:
            for zz in range(4):
                receive(("lc", zz))
        project(4, half)
        sum_send(half, half, 0)
        project(3, half)
        sum_send(0, half, 1)
        project(5, half)
        sum_send(1, half, 1)
    yield "hidden_wait_1"
    hidden_wait(1)
    yield "sum_1"
    for half in (0, 1):
        project(2, half)
        project(6, half)
        sum_send(0, half, 2)
        sum_send(1, half, 2)
    yield "sum_2"
    for half in (0, 1):
        project(1, half)
        project(7, half)
        sum_send(0, half, 3)
        sum_send(1, half, 3)
    for half in (0, 1):
        project(0, half)

    row = lax.broadcasted_iota(jnp.int32, (256, 256), 0)
    column = lax.broadcasted_iota(jnp.int32, (256, 256), 1)
    swapped = (row // 128) * 32 + ((row // 64) % 2) * 64 + ((row // 32) % 2) * 128 + row % 32
    order = jnp.where(swapped == column, 1.0, 0.0).astype(BF)
    loaded("mom1")
    loaded("mom2")
    n1[...] = jnp.dot(m1[...], order, preferred_element_type=F32)
    n2[...] = jnp.dot(m2[...], order, preferred_element_type=F32)

    def gather_x(half, which, source, lanes):
        ref = dr.at[source, :, lanes]
        for k, (sx, dev) in enumerate(xpeers):
            send(rcopy(ref, ref, dx_s.at[half, which, k], dx_r.at[half, source], dev))
            peer = source - x + sx
            expect(("dx", half, which, k), landing(dr.at[peer, :, lanes], dx_r.at[half, peer]))

    other = (1 - zh) * 4 + x
    lane_sets = []
    for half in (0, 1):
        yield "sum_end_%d" % half
        value = part[0, half]
        for direction in (0, 1):
            receive(("sum", direction, half, 3))
            value = value + arrived[direction, half, 3].astype(F32)
        lanes = pl.ds(pl.multiple_of((c if half == 0 else 1 - c) * 128, 128), 128)
        lane_sets.append(lanes)
        first_f = 0.9 * n1[:, lanes] + 0.1 * value
        second_f = 0.999 * n2[:, lanes] + 0.001 * value * value
        dr[rank, :, lanes] = (first_f / FIRST_FIX / (jnp.sqrt(second_f / SECOND_FIX) + 1e-08)).astype(BF)
        send(rcopy(dr.at[rank, :, lanes], dr.at[rank, :, lanes], dz_s.at[half], dz_r.at[half], partner))
        expect(("dz", half), landing(dr.at[other, :, lanes], dz_r.at[half]))
        gather_x(half, 0, rank, lanes)
        n1[:, lanes] = first_f
        n2[:, lanes] = second_f

    new1[...] = jnp.dot(n1[...].astype(BF), order, preferred_element_type=F32).astype(BF)
    new2[...] = jnp.dot(n2[...].astype(BF), order, preferred_element_type=F32).astype(BF)
    yield "dir_z_wait"
    for half in (0, 1):
        receive(("dz", half))
        gather_x(half, 1, other, lane_sets[half])
    yield "rest"
    for k in range(7):
        receive(("p2", k))
    core_send(1)
    receive(("pc", 0))
    receive(("pc", 1))
    yield "dir_x_wait"

    def update(which, finish):
        for half in (0, 1):
            for k in range(3):
                receive(("dx", half, which, k))
        begin = (zh if which == 0 else 1 - zh) * 4

        def columns(n, carry):
            lanes = pl.ds(pl.multiple_of(n * 256, 256), 256)
            total = acc[n] if finish else jnp.zeros((224, 256), F32)
            for r in range(4):
                rows = p_t[begin + r, :, :, :, lanes].reshape(256, 256)
                total = total + jnp.dot(dr[begin + r], rows, preferred_element_type=F32)
            if finish:
                upd_v[:, lanes] = total.astype(BF)
                pltpu.make_async_copy(upd_v.at[:, lanes], upd.at[:, lanes], out_sem.at[n]).start()
            else:
                acc[n] = total
            return carry

        lax.fori_loop(0, 4, columns, 0)

    yield "update_0"
    update(0, False)
    yield "update_1"
    update(1, True)
    for n in range(4):
        lanes = pl.ds(n * 256, 256)
        pltpu.make_async_copy(upd_v.at[:, lanes], upd.at[:, lanes], out_sem.at[n]).wait()


def hand_over(*refs):
    for k in range(3):
        refs[3 + k][...] = refs[k][...]


def per_device(cotangents, hidden, projector, moment_first, moment_second):
    dma = pltpu.SemaphoreType.DMA
    vmem = pl.BlockSpec(memory_space=pltpu.VMEM)
    anywhere = pl.BlockSpec(memory_space=pl.ANY)
    shapes = (
        jax.ShapeDtypeStruct((224, 1024), BF),
        jax.ShapeDtypeStruct((224, 256), BF),
        jax.ShapeDtypeStruct((224, 256), BF),
    )
    results = pl.pallas_call(
        kernel,
        out_shape=shapes,
        in_specs=[anywhere] * 5,
        out_specs=(anywhere, vmem, vmem),
        scratch_shapes=[
            pltpu.VMEM((128, 14336), BF),
            pltpu.VMEM((128, 1024), BF),
            pltpu.VMEM((8, 1792, 128), BF),
            pltpu.VMEM((8, 224, 1024), BF),
            pltpu.VMEM((8, 2, 2, 64, 1024), BF),
            pltpu.VMEM((1024, 512), BF),
            pltpu.VMEM((8, 64, 512), BF),
            pltpu.VMEM((4, 2, 64, 512), BF),
            pltpu.VMEM((64, 512), BF),
            pltpu.VMEM((64, 512), BF),
            pltpu.VMEM((2, 2, 2, 64, 512), BF),
            pltpu.VMEM((8, 2, 224, 128), F32),
            pltpu.VMEM((2, 2, 4, 224, 128), BF),
            pltpu.VMEM((2, 2, 4, 224, 128), BF),
            pltpu.VMEM((8, 224, 256), BF),
            pltpu.VMEM((224, 256), BF),
            pltpu.VMEM((224, 256), BF),
            pltpu.VMEM((224, 256), F32),
            pltpu.VMEM((224, 256), F32),
            pltpu.VMEM((4, 224, 256), F32),
            pltpu.VMEM((224, 1024), BF),
            dma((6,)),
            dma((4,)),
            dma((4,)), dma((4,)),
            dma((3,)), dma((3,)),
            dma((2, 2, 4)), dma((2, 2, 4)),
            dma((2, 3, 2)), dma((2, 6)),
            dma((2, 4)), dma((2, 4)),
            dma, dma,
            dma((8,)), dma((4, 2)),
            dma, dma,
            dma((3,)), dma((4,)),
            dma((4,)), dma((4,)),
            dma((7,)), dma((7,)),
            dma((2,)), dma((2,)),
            dma((2, 2, 4)), dma((2, 2, 4)),
            dma((2,)), dma((2,)),
            dma((2, 2, 3)), dma((2, 8)),
        ],
        compiler_params=pltpu.CompilerParams(
            collective_id=0, has_side_effects=True, vmem_limit_bytes=VL * 2**20
        ),
        cost_estimate=pl.CostEstimate(flops=2_500_000_000, bytes_accessed=6_000_000, transcendentals=60_000),
        name="galore",
    )(cotangents, hidden, projector.T, moment_first.T, moment_second.T)
    results = pl.pallas_call(
        hand_over,
        out_shape=shapes,
        in_specs=[vmem] * 3,
        out_specs=(vmem,) * 3,
        cost_estimate=pl.CostEstimate(flops=0, bytes_accessed=1_400_000, transcendentals=0),
        name="hand_over",
    )(*results)
    return tuple(array.T for array in results)


def solution(mesh):
    return jax.shard_map(
        per_device,
        mesh=mesh,
        in_specs=(
            P("fsdp", "rank"),
            P("fsdp", None),
            P("rank", "fsdp"),
            P("rank", "fsdp"),
            P("rank", "fsdp"),
        ),
        out_specs=(P("rank", "fsdp"), P("rank", "fsdp"), P("rank", "fsdp")),
        check_vma=False,
    )
```

```python
import jax
import jax.numpy as jnp
from jax import lax
from jax.experimental import pallas as pl
from jax.experimental.pallas import tpu as pltpu
from jax.sharding import PartitionSpec as P

STEP = 20
FIRST_FIX = 1.0 - 0.9**STEP
SECOND_FIX = 1.0 - 0.999**STEP
BF = jnp.bfloat16
F32 = jnp.float32
MESH = pl.DeviceIdType.MESH
STOP = None
VL = 60


def guarded(when, act):
    if when is None:
        act()
    else:
        pl.when(when)(act)


def kernel(*refs):
    state = {"in": {}, "out": [], "local": {}}
    for name in body(state, *refs):
        if name == STOP:
            break
    for copy in list(state["local"].values()):
        copy.wait()
    for copy, when in list(state["in"].values()):
        guarded(when, copy.wait_recv)
    for copy, when in state["out"]:
        guarded(when, copy.wait_send)


def body(
    state, cot, hid, prj, mom1, mom2,
    upd, new1, new2,
    hid_v, cot_v, hid_t, hbuf, p_t, cot_t, xs, xb, zs, zb, lt, part, stage, arrived, dr, m1, m2, n1, n2, acc, upd_v,
    loc_sem, out_sem,
    pp_s, pp_r, ct_s, ct_r, ring_s, ring_r, hz_s, hz_r, hx_s, hx_r, hs_s, hs_r,
    ls_s, ls_r, lz_s, lz_r, lg_s, lg_r, lc_s, lc_r, p2_s, p2_r, pc_s, pc_r,
    rs_s, rs_r, dz_s, dz_r, dx_s, dx_r,
):
    inbox, outbox, local = state["in"], state["out"], state["local"]

    def send(copy, when=None):
        guarded(when, copy.start)
        outbox.append((copy, when))

    def expect(key, copy, when=None):
        inbox[key] = (copy, when)

    def receive(key):
        copy, when = inbox.pop(key)
        guarded(when, copy.wait_recv)

    def load(key, copy):
        copy.start()
        local[key] = copy

    def loaded(key):
        local.pop(key).wait()

    rank = lax.axis_index("rank")
    shard = lax.axis_index("fsdp")
    zh, x = rank // 4, rank % 4
    y, zl, c = shard // 8, (shard // 2) % 4, shard % 2
    z = zh * 4 + zl
    low, high = zl % 2, zl // 2

    def at(zh_, x_, y_, zl_, c_):
        return (zh_ * 4 + x_, y_ * 8 + zl_ * 2 + c_)

    def at_z(z_, c_):
        return at(z_ // 4, x, y, z_ % 4, c_)

    def at_y(step):
        return at(zh, x, (y + step + 8) % 8, zl, c)

    def rcopy(src, dst, ssem, rsem, dev):
        return pltpu.make_async_remote_copy(
            src_ref=src, dst_ref=dst, send_sem=ssem, recv_sem=rsem, device_id=dev, device_id_type=MESH
        )

    def landing(ref, sem):
        return rcopy(ref, ref, hs_s, sem, sibling)

    sibling = at(zh, x, y, zl, 1 - c)
    partner = at(1 - zh, x, y, zl, c)
    xpeers = [((x + k) % 4, at(zh, (x + k) % 4, y, zl, c)) for k in (1, 2, 3)]
    zpeers = [((zl + k) % 4, at(zh, x, y, (zl + k) % 4, c)) for k in (1, 2, 3)]

    def shard_ref(block, lo, hi):
        return p_t.at[block, c, lo, pl.ds(pl.multiple_of(hi * 32, 32), 32)]

    yield "start"
    load("prj", pltpu.make_async_copy(prj, shard_ref(y, low, high), loc_sem.at[0]))
    load("cot", pltpu.make_async_copy(cot, cot_v, loc_sem.at[1]))
    load("hid", pltpu.make_async_copy(hid, hid_v, loc_sem.at[2]))
    load("mom1", pltpu.make_async_copy(mom1, m1, loc_sem.at[3]))
    load("mom2", pltpu.make_async_copy(mom2, m2, loc_sem.at[4]))

    barrier = pltpu.get_barrier_semaphore()
    greet = [sibling, partner] + [d for _, d in xpeers] + [d for _, d in zpeers]
    greet += [at_y(1), at_y(-1), at_y(2), at_y(-2)]
    greet += [at_z((z + off) % 8, cc) for off in (1, 7, 2, 6) for cc in (0, 1)]
    for dev in greet:
        pl.semaphore_signal(barrier, inc=1, device_id=dev, device_id_type=MESH)

    def cot_ref(lo, cc):
        return cot_t.at[:, pl.ds(pl.multiple_of(lo * 256 + cc * 128, 128), 128)]

    loaded("cot")
    cot_t[:, pl.ds(pl.multiple_of(low * 256 + c * 128, 128), 128)] = cot_v[...].T
    loaded("prj")
    yield "barrier"
    pl.semaphore_wait(barrier, len(greet))
    yield "first_sends"

    def ring_ref(block, kind):
        return shard_ref(block, low, high if kind == 0 else 1 - high)

    def ring_send(direction, kind, step):
        sign = 1 - 2 * direction
        sems = ring_s.at[direction, kind, step], ring_r.at[direction, kind, step]
        origin = (y - sign * min(step, 2) + 8) % 8
        ref = ring_ref(origin, kind)
        send(rcopy(ref, ref, *sems, at_y(sign * (2 if step == 3 else 1))))

    def ring_expect(direction, kind, step):
        origin = (y - (1 - 2 * direction) * (step + 1) + 8) % 8
        expect(("ring", direction, kind, step), landing(ring_ref(origin, kind), ring_r.at[direction, kind, step]))

    own_shard = ring_ref(y, 0)

    def shard_send(k):
        zz, dev = zpeers[k - 1]
        send(rcopy(own_shard, own_shard, pp_s.at[k], pp_r.at[k], dev))
        source = (zl + 4 - k) % 4
        expect(("pp", k), landing(shard_ref(y, source % 2, source // 2), pp_r.at[k]))

    shard_send(2)
    for direction in (0, 1):
        ring_send(direction, 0, 0)
        for kind in (0, 1):
            ring_expect(direction, kind, 0)

    def cot_send(ref, k, dev):
        send(rcopy(ref, ref, ct_s.at[k], ct_r.at[k], dev))

    cot_send(cot_ref(low, c), 1, sibling)
    expect("cot1", landing(cot_ref(low, 1 - c), ct_r.at[1]))

    def transpose_block(block):
        def tile(t, carry):
            column = pl.multiple_of(block * 1792 + t * 128, 128)
            row = pl.multiple_of(t * 128, 128)
            hid_t[block, pl.ds(row, 128), :] = hid_v[:, pl.ds(column, 128)].T
            return carry

        lax.fori_loop(0, 14, tile, 0, unroll=7)

    def fetched(position, rnd):
        first = jnp.where(position == 0, 4, jnp.where(position == 1, 3, jnp.where(position == 2, 5, 2)))
        return (y + first + 4 * rnd) % 8

    blocks = [fetched(x, rnd) for rnd in (0, 1)]

    def hidden_send(rnd):
        block = blocks[rnd]
        for k, (off, rot) in enumerate(((1, 3), (7, 1), (None, 2))):
            zd = (z + off) % 8 if off is not None else (z + 2 + 4 * c) % 8
            lane = pl.multiple_of(rot * 256 + c * 128, 128)
            for cc in (0, 1):
                row = pl.multiple_of((2 * (zd % 4) + cc) * 224, 16)
                send(rcopy(
                    hid_t.at[block, pl.ds(row, 224)], hbuf.at[block, :, pl.ds(lane, 128)],
                    hz_s.at[rnd, k, cc], hz_r.at[rnd, 2 * k + c], at_z(zd, cc),
                ))
                ref = hbuf.at[block, :, pl.ds(rot * 256 + cc * 128, 128)]
                expect(("hz", rnd, k, cc), landing(ref, hz_r.at[rnd, 2 * k + cc]))

    def hidden_forward(rnd):
        for k in range(3):
            for cc in (0, 1):
                receive(("hz", rnd, k, cc))
        for side in (0, 1):
            near = fetched((x + 3 + 2 * side) % 4, rnd)
            for half in (side, 1 - side):
                rows = pl.ds(half * 112, 112)
                ref = hbuf.at[blocks[rnd], rows, pl.ds(256, 768)]
                sems = hx_s.at[rnd, side, half], hx_r.at[rnd, side, half]
                send(rcopy(ref, ref, *sems, xpeers[2 * side][1]))
                expect(("hx", rnd, side, half), landing(hbuf.at[near, rows, pl.ds(256, 768)], sems[1]))

    def hidden_further(rnd):
        far = fetched((x + 2) % 4, rnd)
        for side in (0, 1):
            receive(("hx", rnd, side, side))
            near = fetched((x + 3 + 2 * side) % 4, rnd)
            rows = pl.ds(side * 112, 112)
            ref = hbuf.at[near, rows, pl.ds(256, 768)]
            sems = hx_s.at[rnd, side, 2], hx_r.at[rnd, side, 2]
            send(rcopy(ref, ref, *sems, xpeers[2 * side][1]))
            expect(("hx", rnd, side, 2), landing(hbuf.at[far, rows, pl.ds(256, 768)], sems[1]))

    def hidden_wait(rnd):
        for side in (0, 1):
            receive(("hx", rnd, side, 1 - side))
            receive(("hx", rnd, side, 2))

    def ring_pass(direction, kind, step):
        receive(("ring", direction, kind, step))
        ring_send(direction, kind, step + 1)
        ring_expect(direction, kind, step + 1)
        if step == 1 and kind == direction:
            ring_send(direction, kind, 3)
            ring_expect(direction, kind, 3)

    yield "hidden_sends"
    loaded("hid")
    transpose_block(blocks[0])
    hidden_send(0)
    transpose_block(blocks[1])
    yield "pair"
    cot_send(cot_ref(low, c), 0, at(zh, x, y, zl + 1 - 2 * low, c))
    expect("cot0", landing(cot_ref(1 - low, c), ct_r.at[0]))
    receive(("pp", 2))
    for direction in (0, 1):
        ring_send(direction, 1, 0)
    yield "ring_0"
    ring_pass(0, 0, 0)
    ring_pass(1, 0, 0)
    for k in range(1, 4):
        transpose_block((blocks[0] + k) % 8)
    yield "ring_0_1"
    ring_pass(0, 1, 0)
    ring_pass(1, 1, 0)
    ring_pass(0, 0, 1)
    ring_pass(1, 0, 1)
    hidden_send(1)
    for k in range(5, 8):
        transpose_block((blocks[0] + k) % 8)
    yield "hidden_forward_0"
    hidden_forward(0)
    yield "ring_1_1"
    ring_pass(0, 1, 1)
    ring_pass(1, 1, 1)

    hs_lane = pl.ds(pl.multiple_of(c * 128, 128), 128)
    load("own", pltpu.make_async_copy(
        hid_t.at[:, pl.ds(pl.multiple_of((2 * zl + c) * 224, 16), 224)], hbuf.at[:, :, hs_lane], loc_sem.at[5]
    ))
    send(rcopy(
        hid_t.at[:, pl.ds(pl.multiple_of((2 * zl + 1 - c) * 224, 16), 224)], hbuf.at[:, :, hs_lane], hs_s, hs_r, sibling
    ))
    expect("hs", landing(hbuf.at[:, :, pl.ds(pl.multiple_of((1 - c) * 128, 128), 128)], hs_r))
    yield "cot_wait"
    receive("cot0")
    cot_send(cot_ref(1 - low, c), 2, sibling)
    expect("cot2", landing(cot_ref(1 - low, 1 - c), ct_r.at[2]))
    receive("cot1")
    receive("cot2")
    shard_send(1)
    shard_send(3)

    def left_block(block):
        rows = p_t[block, c, low]
        xs[block] = jnp.dot(rows, cot_t[...], preferred_element_type=F32).astype(BF)
        send(rcopy(
            xs.at[block], xb.at[x, block // 4], ls_s.at[block], ls_r.at[x, block // 4], at(zh, block % 4, y, zl, c)
        ), block % 4 != x)

    yield "left_first"
    for distance in (0, 1, 7, 2, 6):
        left_block((y + distance) % 8)

    yield "ring_2"
    for kind in (0, 1):
        for direction in (0, 1):
            receive(("ring", direction, kind, 2))
    left_block((y + 3) % 8)
    left_block((y + 5) % 8)
    yield "ring_3"
    receive(("ring", 0, 0, 3))
    receive(("ring", 1, 1, 3))
    left_block((y + 4) % 8)

    def rest_send_y():
        for direction in (0, 1):
            sign = 1 - 2 * direction
            ref = p_t.at[y, c, 1 - low]
            send(rcopy(ref, ref, p2_s.at[direction], p2_r.at[direction], at_y(sign)))
            expect(("p2", direction), landing(p_t.at[(y - sign + 8) % 8, c, 1 - low], p2_r.at[direction]))

    def core_send(k):
        lo = low if k == 0 else 1 - low
        ref = p_t.at[:, c, lo]
        send(rcopy(ref, ref, pc_s.at[k], pc_r.at[k], sibling))
        expect(("pc", k), landing(p_t.at[:, 1 - c, lo], pc_r.at[k]))

    def rest_send_z():
        for k in range(2, 7):
            ref = p_t.at[(y + k) % 8, c, low]
            send(rcopy(ref, ref, p2_s.at[k], p2_r.at[k], at(zh, x, y, zl + 1 - 2 * low, c)))
            expect(("p2", k), landing(p_t.at[(y + k) % 8, c, 1 - low], p2_r.at[k]))

    yield "hidden_further_0"
    hidden_further(0)

    def left_wait(side):
        for k in range(3):
            receive(("ls", k, side))

    def left_sum(half):
        total = xs[half * 4 + x].astype(F32)
        for sx, _ in xpeers:
            total = total + xb[sx, half].astype(F32)
        return total

    for k, (sx, _) in enumerate(xpeers):
        for side, half in enumerate((zh, 1 - zh)):
            expect(("ls", k, side), landing(xb.at[sx, half], ls_r.at[sx, half]))

    yield "left_x_wait"
    left_wait(1)
    zs[...] = left_sum(1 - zh).astype(BF)
    send(rcopy(zs, zb, lz_s, lz_r, partner))
    expect("lz", landing(zb, lz_r))
    yield "hidden_forward_1"
    hidden_forward(1)
    yield "rest_0"
    receive(("pp", 1))
    receive(("pp", 3))
    rest_send_y()
    left_wait(0)
    yield "left_z_wait"
    receive("lz")
    mine = lt.at[high, c, low]
    lt[high, c, low] = (left_sum(zh) + zb[...].astype(F32)).astype(BF)
    for k, (zz, dev) in enumerate(zpeers):
        send(rcopy(mine, mine, lg_s.at[k], lg_r.at[zl], dev))
        expect(("lg", k), landing(lt.at[zz // 2, c, zz % 2], lg_r.at[zz]))
    send(rcopy(mine, mine, lc_s.at[zl], lc_r.at[zl], sibling))
    expect(("lc", 0), landing(lt.at[high, 1 - c, low], lc_r.at[zl]))
    yield "hidden_further_1"
    hidden_further(1)
    yield "left_gather"
    for k, (zz, _) in enumerate(zpeers):
        receive(("lg", k))
        ref = lt.at[zz // 2, c, zz % 2]
        send(rcopy(ref, ref, lc_s.at[zz], lc_r.at[zz], sibling))
        expect(("lc", k + 1), landing(lt.at[zz // 2, 1 - c, zz % 2], lc_r.at[zz]))

    rest_send_z()
    core_send(0)
    yield "hidden_local"
    loaded("own")
    receive("hs")

    def project(distance, half):
        block = (y + distance) % 8
        cc = c if half == 0 else 1 - c
        total = jnp.zeros((224, 128), F32)
        for b in range(4):
            zz = (zl + b) % 4
            weights = lt[zz // 2, cc, :, :, pl.ds(pl.multiple_of((zz % 2) * 256, 256), 256)].reshape(128, 256)
            total = total + lax.dot_general(
                hbuf[block, :, b * 256 : b * 256 + 256], weights,
                (((1,), (1,)), ((), ())), preferred_element_type=F32,
            )
        part[distance, half] = total

    def sum_copy(direction, half, step):
        sign = 1 - 2 * direction
        return rcopy(
            stage.at[direction, half, step], arrived.at[direction, half, step],
            rs_s.at[direction, half, step], rs_r.at[direction, half, step], at_y(sign * (2 if step == 0 else 1)),
        )

    def sum_send(direction, half, step):
        distance = 4 - step if direction == 0 else 4 + step
        value = part[distance, half]
        sources = [1] + ([0] if half == direction else []) if step == 2 else [2] if step == 3 else []
        for source in sources:
            receive(("sum", direction, half, source))
            value = value + arrived[direction, half, source].astype(F32)
        stage[direction, half, step] = value.astype(BF)
        copy = sum_copy(direction, half, step)
        send(copy)
        expect(("sum", direction, half, step), copy)

    yield "hidden_wait_0"
    hidden_wait(0)
    yield "sum_0"
    for half in (0, 1):
        if half == 1:
            for zz in range(4):
                receive(("lc", zz))
        project(4, half)
        sum_send(half, half, 0)
        project(3, half)
        sum_send(0, half, 1)
        project(5, half)
        sum_send(1, half, 1)
    yield "hidden_wait_1"
    hidden_wait(1)
    yield "sum_1"
    for half in (0, 1):
        project(2, half)
        project(6, half)
        sum_send(0, half, 2)
        sum_send(1, half, 2)
    yield "sum_2"
    for half in (0, 1):
        project(1, half)
        project(7, half)
        sum_send(0, half, 3)
        sum_send(1, half, 3)
    for half in (0, 1):
        project(0, half)

    row = lax.broadcasted_iota(jnp.int32, (256, 256), 0)
    column = lax.broadcasted_iota(jnp.int32, (256, 256), 1)
    swapped = (row // 128) * 32 + ((row // 64) % 2) * 64 + ((row // 32) % 2) * 128 + row % 32
    order = jnp.where(swapped == column, 1.0, 0.0).astype(BF)
    loaded("mom1")
    loaded("mom2")
    n1[...] = jnp.dot(m1[...], order, preferred_element_type=F32)
    n2[...] = jnp.dot(m2[...], order, preferred_element_type=F32)

    def gather_x(half, which, source, lanes):
        ref = dr.at[source, :, lanes]
        for k, (sx, dev) in enumerate(xpeers):
            send(rcopy(ref, ref, dx_s.at[half, which, k], dx_r.at[half, source], dev))
            peer = source - x + sx
            expect(("dx", half, which, k), landing(dr.at[peer, :, lanes], dx_r.at[half, peer]))

    other = (1 - zh) * 4 + x
    lane_sets = []
    for half in (0, 1):
        yield "sum_end_%d" % half
        value = part[0, half]
        for direction in (0, 1):
            receive(("sum", direction, half, 3))
            value = value + arrived[direction, half, 3].astype(F32)
        lanes = pl.ds(pl.multiple_of((c if half == 0 else 1 - c) * 128, 128), 128)
        lane_sets.append(lanes)
        first_f = 0.9 * n1[:, lanes] + 0.1 * value
        second_f = 0.999 * n2[:, lanes] + 0.001 * value * value
        dr[rank, :, lanes] = (first_f / FIRST_FIX / (jnp.sqrt(second_f / SECOND_FIX) + 1e-08)).astype(BF)
        send(rcopy(dr.at[rank, :, lanes], dr.at[rank, :, lanes], dz_s.at[half], dz_r.at[half], partner))
        expect(("dz", half), landing(dr.at[other, :, lanes], dz_r.at[half]))
        gather_x(half, 0, rank, lanes)
        n1[:, lanes] = first_f
        n2[:, lanes] = second_f

    m1[...] = jnp.dot(n1[...].astype(BF), order, preferred_element_type=F32).astype(BF)
    m2[...] = jnp.dot(n2[...].astype(BF), order, preferred_element_type=F32).astype(BF)
    load("new1", pltpu.make_async_copy(m1, new1, out_sem.at[4]))
    load("new2", pltpu.make_async_copy(m2, new2, out_sem.at[5]))
    yield "dir_z_wait"
    for half in (0, 1):
        receive(("dz", half))
        gather_x(half, 1, other, lane_sets[half])
    yield "rest"
    for k in range(7):
        receive(("p2", k))
    core_send(1)
    receive(("pc", 0))
    receive(("pc", 1))
    yield "dir_x_wait"

    def update(which, finish):
        for half in (0, 1):
            for k in range(3):
                receive(("dx", half, which, k))
        begin = (zh if which == 0 else 1 - zh) * 4

        def columns(n, carry):
            lanes = pl.ds(pl.multiple_of(n * 256, 256), 256)
            total = acc[n] if finish else jnp.zeros((224, 256), F32)
            for r in range(4):
                rows = p_t[begin + r, :, :, :, lanes].reshape(256, 256)
                total = total + jnp.dot(dr[begin + r], rows, preferred_element_type=F32)
            if finish:
                upd_v[:, lanes] = total.astype(BF)
                pltpu.make_async_copy(upd_v.at[:, lanes], upd.at[:, lanes], out_sem.at[n]).start()
            else:
                acc[n] = total
            return carry

        lax.fori_loop(0, 4, columns, 0)

    yield "update_0"
    update(0, False)
    yield "update_1"
    update(1, True)
    for n in range(4):
        lanes = pl.ds(n * 256, 256)
        pltpu.make_async_copy(upd_v.at[:, lanes], upd.at[:, lanes], out_sem.at[n]).wait()


def hand_over(*refs):
    sems = refs[9]
    reads = [pltpu.make_async_copy(refs[k], refs[6 + k], sems.at[0, k]) for k in range(3)]
    writes = [pltpu.make_async_copy(refs[6 + k], refs[3 + k], sems.at[1, k]) for k in range(3)]
    for copy in reads:
        copy.start()
    for read, write in zip(reads, writes):
        read.wait()
        write.start()
    for copy in writes:
        copy.wait()


def per_device(cotangents, hidden, projector, moment_first, moment_second):
    dma = pltpu.SemaphoreType.DMA
    anywhere = pl.BlockSpec(memory_space=pl.ANY)
    shapes = (
        jax.ShapeDtypeStruct((224, 1024), BF),
        jax.ShapeDtypeStruct((224, 256), BF),
        jax.ShapeDtypeStruct((224, 256), BF),
    )
    results = pl.pallas_call(
        kernel,
        out_shape=shapes,
        in_specs=[anywhere] * 5,
        out_specs=(anywhere, anywhere, anywhere),
        scratch_shapes=[
            pltpu.VMEM((128, 14336), BF),
            pltpu.VMEM((128, 1024), BF),
            pltpu.VMEM((8, 1792, 128), BF),
            pltpu.VMEM((8, 224, 1024), BF),
            pltpu.VMEM((8, 2, 2, 64, 1024), BF),
            pltpu.VMEM((1024, 512), BF),
            pltpu.VMEM((8, 64, 512), BF),
            pltpu.VMEM((4, 2, 64, 512), BF),
            pltpu.VMEM((64, 512), BF),
            pltpu.VMEM((64, 512), BF),
            pltpu.VMEM((2, 2, 2, 64, 512), BF),
            pltpu.VMEM((8, 2, 224, 128), F32),
            pltpu.VMEM((2, 2, 4, 224, 128), BF),
            pltpu.VMEM((2, 2, 4, 224, 128), BF),
            pltpu.VMEM((8, 224, 256), BF),
            pltpu.VMEM((224, 256), BF),
            pltpu.VMEM((224, 256), BF),
            pltpu.VMEM((224, 256), F32),
            pltpu.VMEM((224, 256), F32),
            pltpu.VMEM((4, 224, 256), F32),
            pltpu.VMEM((224, 1024), BF),
            dma((6,)),
            dma((6,)),
            dma((4,)), dma((4,)),
            dma((3,)), dma((3,)),
            dma((2, 2, 4)), dma((2, 2, 4)),
            dma((2, 3, 2)), dma((2, 6)),
            dma((2, 2, 3)), dma((2, 2, 3)),
            dma, dma,
            dma((8,)), dma((4, 2)),
            dma, dma,
            dma((3,)), dma((4,)),
            dma((4,)), dma((4,)),
            dma((7,)), dma((7,)),
            dma((2,)), dma((2,)),
            dma((2, 2, 4)), dma((2, 2, 4)),
            dma((2,)), dma((2,)),
            dma((2, 2, 3)), dma((2, 8)),
        ],
        compiler_params=pltpu.CompilerParams(
            collective_id=0, has_side_effects=True, vmem_limit_bytes=VL * 2**20
        ),
        cost_estimate=pl.CostEstimate(flops=2_500_000_000, bytes_accessed=6_000_000, transcendentals=60_000),
        name="galore",
    )(cotangents, hidden, projector.T, moment_first.T, moment_second.T)
    results = pl.pallas_call(
        hand_over,
        out_shape=shapes,
        in_specs=[anywhere] * 3,
        out_specs=(anywhere,) * 3,
        scratch_shapes=[pltpu.VMEM(shape.shape, BF) for shape in shapes] + [dma((2, 3))],
        cost_estimate=pl.CostEstimate(flops=0, bytes_accessed=1_400_000, transcendentals=0),
        name="hand_over",
    )(*results)
    return tuple(array.T for array in results)


def solution(mesh):
    return jax.shard_map(
        per_device,
        mesh=mesh,
        in_specs=(
            P("fsdp", "rank"),
            P("fsdp", None),
            P("rank", "fsdp"),
            P("rank", "fsdp"),
            P("rank", "fsdp"),
        ),
        out_specs=(P("rank", "fsdp"), P("rank", "fsdp"), P("rank", "fsdp")),
        check_vma=False,
    )
```

```python
import jax
import jax.numpy as jnp
from jax import lax
from jax.experimental import pallas as pl
from jax.experimental.pallas import tpu as pltpu
from jax.sharding import PartitionSpec as P

STEP = 20
FIRST_FIX = 1.0 - 0.9**STEP
SECOND_FIX = 1.0 - 0.999**STEP
BF = jnp.bfloat16
F32 = jnp.float32
MESH = pl.DeviceIdType.MESH
STOP = None
VL = 60


def guarded(when, act):
    if when is None:
        act()
    else:
        pl.when(when)(act)


def kernel(*refs):
    state = {"in": {}, "out": [], "local": {}}
    for name in body(state, *refs):
        if name == STOP:
            break
    for copy in list(state["local"].values()):
        copy.wait()
    for copy, when in list(state["in"].values()):
        guarded(when, copy.wait_recv)
    for copy, when in state["out"]:
        guarded(when, copy.wait_send)


def body(
    state, cot, hid, prj, mom1, mom2,
    upd, new1, new2,
    hid_v, cot_v, hid_t, hbuf, p_t, cot_t, xs, xb, zs, zb, lt, part, stage, arrived, dr, m1, m2, n1, n2, acc, upd_v,
    loc_sem, out_sem,
    pp_s, pp_r, ct_s, ct_r, ring_s, ring_r, hz_s, hz_r, hx_s, hx_r, hs_s, hs_r,
    ls_s, ls_r, lz_s, lz_r, lg_s, lg_r, lc_s, lc_r, p2_s, p2_r, pc_s, pc_r,
    rs_s, rs_r, dz_s, dz_r, dx_s, dx_r,
):
    inbox, outbox, local = state["in"], state["out"], state["local"]

    def send(copy, when=None):
        guarded(when, copy.start)
        outbox.append((copy, when))

    def expect(key, copy, when=None):
        inbox[key] = (copy, when)

    def receive(key):
        copy, when = inbox.pop(key)
        guarded(when, copy.wait_recv)

    def load(key, copy):
        copy.start()
        local[key] = copy

    def loaded(key):
        local.pop(key).wait()

    rank = lax.axis_index("rank")
    shard = lax.axis_index("fsdp")
    zh, x = rank // 4, rank % 4
    y, zl, c = shard // 8, (shard // 2) % 4, shard % 2
    z = zh * 4 + zl
    low, high = zl % 2, zl // 2

    def at(zh_, x_, y_, zl_, c_):
        return (zh_ * 4 + x_, y_ * 8 + zl_ * 2 + c_)

    def at_z(z_, c_):
        return at(z_ // 4, x, y, z_ % 4, c_)

    def at_y(step):
        return at(zh, x, (y + step + 8) % 8, zl, c)

    def rcopy(src, dst, ssem, rsem, dev):
        return pltpu.make_async_remote_copy(
            src_ref=src, dst_ref=dst, send_sem=ssem, recv_sem=rsem, device_id=dev, device_id_type=MESH
        )

    def landing(ref, sem):
        return rcopy(ref, ref, hs_s, sem, sibling)

    sibling = at(zh, x, y, zl, 1 - c)
    partner = at(1 - zh, x, y, zl, c)
    xpeers = [((x + k) % 4, at(zh, (x + k) % 4, y, zl, c)) for k in (1, 2, 3)]
    zpeers = [((zl + k) % 4, at(zh, x, y, (zl + k) % 4, c)) for k in (1, 2, 3)]

    def shard_ref(block, lo, hi):
        return p_t.at[block, c, lo, pl.ds(pl.multiple_of(hi * 32, 32), 32)]

    yield "start"
    load("prj", pltpu.make_async_copy(prj, shard_ref(y, low, high), loc_sem.at[0]))
    load("cot", pltpu.make_async_copy(cot, cot_v, loc_sem.at[1]))
    load("hid", pltpu.make_async_copy(hid, hid_v, loc_sem.at[2]))
    load("mom1", pltpu.make_async_copy(mom1, m1, loc_sem.at[3]))
    load("mom2", pltpu.make_async_copy(mom2, m2, loc_sem.at[4]))

    barrier = pltpu.get_barrier_semaphore()
    greet = [sibling, partner] + [d for _, d in xpeers] + [d for _, d in zpeers]
    greet += [at_y(1), at_y(-1), at_y(2), at_y(-2)]
    greet += [at_z((z + off) % 8, cc) for off in (1, 7, 2, 6) for cc in (0, 1)]
    for dev in greet:
        pl.semaphore_signal(barrier, inc=1, device_id=dev, device_id_type=MESH)

    def cot_ref(lo, cc):
        return cot_t.at[:, pl.ds(pl.multiple_of(lo * 256 + cc * 128, 128), 128)]

    loaded("cot")
    cot_t[:, pl.ds(pl.multiple_of(low * 256 + c * 128, 128), 128)] = cot_v[...].T
    loaded("prj")
    yield "barrier"
    pl.semaphore_wait(barrier, len(greet))
    yield "first_sends"

    def ring_ref(block, kind):
        return shard_ref(block, low, high if kind == 0 else 1 - high)

    def ring_send(direction, kind, step):
        sign = 1 - 2 * direction
        sems = ring_s.at[direction, kind, step], ring_r.at[direction, kind, step]
        origin = (y - sign * min(step, 2) + 8) % 8
        ref = ring_ref(origin, kind)
        send(rcopy(ref, ref, *sems, at_y(sign * (2 if step == 3 else 1))))

    def ring_expect(direction, kind, step):
        origin = (y - (1 - 2 * direction) * (step + 1) + 8) % 8
        expect(("ring", direction, kind, step), landing(ring_ref(origin, kind), ring_r.at[direction, kind, step]))

    own_shard = ring_ref(y, 0)

    def shard_send(k):
        zz, dev = zpeers[k - 1]
        send(rcopy(own_shard, own_shard, pp_s.at[k], pp_r.at[k], dev))
        source = (zl + 4 - k) % 4
        expect(("pp", k), landing(shard_ref(y, source % 2, source // 2), pp_r.at[k]))

    shard_send(2)
    for direction in (0, 1):
        ring_send(direction, 0, 0)
        for kind in (0, 1):
            ring_expect(direction, kind, 0)

    def cot_send(ref, k, dev):
        send(rcopy(ref, ref, ct_s.at[k], ct_r.at[k], dev))

    cot_send(cot_ref(low, c), 1, sibling)
    expect("cot1", landing(cot_ref(low, 1 - c), ct_r.at[1]))

    def transpose_block(block):
        def tile(t, carry):
            column = pl.multiple_of(block * 1792 + t * 128, 128)
            row = pl.multiple_of(t * 128, 128)
            hid_t[block, pl.ds(row, 128), :] = hid_v[:, pl.ds(column, 128)].T
            return carry

        lax.fori_loop(0, 14, tile, 0, unroll=7)

    def fetched(position, rnd):
        first = jnp.where(position == 0, 4, jnp.where(position == 1, 3, jnp.where(position == 2, 5, 2)))
        return (y + first + 4 * rnd) % 8

    blocks = [fetched(x, rnd) for rnd in (0, 1)]

    def hidden_send(rnd):
        block = blocks[rnd]
        for k, (off, rot) in enumerate(((1, 3), (7, 1), (None, 2))):
            zd = (z + off) % 8 if off is not None else (z + 2 + 4 * c) % 8
            lane = pl.multiple_of(rot * 256 + c * 128, 128)
            for cc in (0, 1):
                row = pl.multiple_of((2 * (zd % 4) + cc) * 224, 16)
                send(rcopy(
                    hid_t.at[block, pl.ds(row, 224)], hbuf.at[block, :, pl.ds(lane, 128)],
                    hz_s.at[rnd, k, cc], hz_r.at[rnd, 2 * k + c], at_z(zd, cc),
                ))
                ref = hbuf.at[block, :, pl.ds(rot * 256 + cc * 128, 128)]
                expect(("hz", rnd, k, cc), landing(ref, hz_r.at[rnd, 2 * k + cc]))

    def hidden_forward(rnd):
        for k in range(3):
            for cc in (0, 1):
                receive(("hz", rnd, k, cc))
        for side in (0, 1):
            near = fetched((x + 3 + 2 * side) % 4, rnd)
            for half in (side, 1 - side):
                rows = pl.ds(half * 112, 112)
                ref = hbuf.at[blocks[rnd], rows, pl.ds(256, 768)]
                sems = hx_s.at[rnd, side, half], hx_r.at[rnd, side, half]
                send(rcopy(ref, ref, *sems, xpeers[2 * side][1]))
                expect(("hx", rnd, side, half), landing(hbuf.at[near, rows, pl.ds(256, 768)], sems[1]))

    def hidden_further(rnd):
        far = fetched((x + 2) % 4, rnd)
        for side in (0, 1):
            receive(("hx", rnd, side, side))
            near = fetched((x + 3 + 2 * side) % 4, rnd)
            rows = pl.ds(side * 112, 112)
            ref = hbuf.at[near, rows, pl.ds(256, 768)]
            sems = hx_s.at[rnd, side, 2], hx_r.at[rnd, side, 2]
            send(rcopy(ref, ref, *sems, xpeers[2 * side][1]))
            expect(("hx", rnd, side, 2), landing(hbuf.at[far, rows, pl.ds(256, 768)], sems[1]))

    def hidden_wait(rnd):
        for side in (0, 1):
            receive(("hx", rnd, side, 1 - side))
            receive(("hx", rnd, side, 2))

    def ring_pass(direction, kind, step):
        receive(("ring", direction, kind, step))
        ring_send(direction, kind, step + 1)
        ring_expect(direction, kind, step + 1)
        if step == 1 and kind == direction:
            ring_send(direction, kind, 3)
            ring_expect(direction, kind, 3)

    yield "hidden_sends"
    loaded("hid")
    transpose_block(blocks[0])
    hidden_send(0)
    transpose_block(blocks[1])
    yield "pair"
    cot_send(cot_ref(low, c), 0, at(zh, x, y, zl + 1 - 2 * low, c))
    expect("cot0", landing(cot_ref(1 - low, c), ct_r.at[0]))
    receive(("pp", 2))
    for direction in (0, 1):
        ring_send(direction, 1, 0)
    yield "ring_0"
    ring_pass(0, 0, 0)
    ring_pass(1, 0, 0)
    for k in range(1, 4):
        transpose_block((blocks[0] + k) % 8)
    yield "ring_0_1"
    ring_pass(0, 1, 0)
    ring_pass(1, 1, 0)
    ring_pass(0, 0, 1)
    ring_pass(1, 0, 1)
    hidden_send(1)
    for k in range(5, 8):
        transpose_block((blocks[0] + k) % 8)
    yield "hidden_forward_0"
    hidden_forward(0)
    yield "ring_1_1"
    ring_pass(0, 1, 1)
    ring_pass(1, 1, 1)

    hs_lane = pl.ds(pl.multiple_of(c * 128, 128), 128)
    load("own", pltpu.make_async_copy(
        hid_t.at[:, pl.ds(pl.multiple_of((2 * zl + c) * 224, 16), 224)], hbuf.at[:, :, hs_lane], loc_sem.at[5]
    ))
    send(rcopy(
        hid_t.at[:, pl.ds(pl.multiple_of((2 * zl + 1 - c) * 224, 16), 224)], hbuf.at[:, :, hs_lane], hs_s, hs_r, sibling
    ))
    expect("hs", landing(hbuf.at[:, :, pl.ds(pl.multiple_of((1 - c) * 128, 128), 128)], hs_r))
    yield "cot_wait"
    receive("cot0")
    cot_send(cot_ref(1 - low, c), 2, sibling)
    expect("cot2", landing(cot_ref(1 - low, 1 - c), ct_r.at[2]))
    receive("cot1")
    receive("cot2")
    shard_send(1)
    shard_send(3)

    def left_block(block):
        rows = p_t[block, c, low]
        xs[block] = jnp.dot(rows, cot_t[...], preferred_element_type=F32).astype(BF)
        send(rcopy(
            xs.at[block], xb.at[x, block // 4], ls_s.at[block], ls_r.at[x, block // 4], at(zh, block % 4, y, zl, c)
        ), block % 4 != x)

    yield "left_first"
    for distance in (0, 1, 7, 2, 6):
        left_block((y + distance) % 8)

    yield "ring_2"
    for kind in (0, 1):
        for direction in (0, 1):
            receive(("ring", direction, kind, 2))
    left_block((y + 3) % 8)
    left_block((y + 5) % 8)
    yield "ring_3"
    receive(("ring", 0, 0, 3))
    receive(("ring", 1, 1, 3))
    left_block((y + 4) % 8)

    def rest_send_y():
        for direction in (0, 1):
            sign = 1 - 2 * direction
            ref = p_t.at[y, c, 1 - low]
            send(rcopy(ref, ref, p2_s.at[direction], p2_r.at[direction], at_y(sign)))
            expect(("p2", direction), landing(p_t.at[(y - sign + 8) % 8, c, 1 - low], p2_r.at[direction]))

    def core_send(k):
        lo = low if k == 0 else 1 - low
        ref = p_t.at[:, c, lo]
        send(rcopy(ref, ref, pc_s.at[k], pc_r.at[k], sibling))
        expect(("pc", k), landing(p_t.at[:, 1 - c, lo], pc_r.at[k]))

    def rest_send_z():
        for k in range(2, 7):
            ref = p_t.at[(y + k) % 8, c, low]
            send(rcopy(ref, ref, p2_s.at[k], p2_r.at[k], at(zh, x, y, zl + 1 - 2 * low, c)))
            expect(("p2", k), landing(p_t.at[(y + k) % 8, c, 1 - low], p2_r.at[k]))

    yield "hidden_further_0"
    hidden_further(0)

    def left_wait(side):
        for k in range(3):
            receive(("ls", k, side))

    def left_sum(half):
        total = xs[half * 4 + x].astype(F32)
        for sx, _ in xpeers:
            total = total + xb[sx, half].astype(F32)
        return total

    for k, (sx, _) in enumerate(xpeers):
        for side, half in enumerate((zh, 1 - zh)):
            expect(("ls", k, side), landing(xb.at[sx, half], ls_r.at[sx, half]))

    yield "left_x_wait"
    left_wait(1)
    zs[...] = left_sum(1 - zh).astype(BF)
    send(rcopy(zs, zb, lz_s, lz_r, partner))
    expect("lz", landing(zb, lz_r))
    yield "hidden_forward_1"
    hidden_forward(1)
    yield "rest_0"
    receive(("pp", 1))
    receive(("pp", 3))
    rest_send_y()
    left_wait(0)
    yield "left_z_wait"
    receive("lz")
    mine = lt.at[high, c, low]
    lt[high, c, low] = (left_sum(zh) + zb[...].astype(F32)).astype(BF)
    for k, (zz, dev) in enumerate(zpeers):
        send(rcopy(mine, mine, lg_s.at[k], lg_r.at[zl], dev))
        expect(("lg", k), landing(lt.at[zz // 2, c, zz % 2], lg_r.at[zz]))
    send(rcopy(mine, mine, lc_s.at[zl], lc_r.at[zl], sibling))
    expect(("lc", 0), landing(lt.at[high, 1 - c, low], lc_r.at[zl]))
    yield "hidden_further_1"
    hidden_further(1)
    yield "left_gather"
    for k, (zz, _) in enumerate(zpeers):
        receive(("lg", k))
        ref = lt.at[zz // 2, c, zz % 2]
        send(rcopy(ref, ref, lc_s.at[zz], lc_r.at[zz], sibling))
        expect(("lc", k + 1), landing(lt.at[zz // 2, 1 - c, zz % 2], lc_r.at[zz]))

    rest_send_z()
    yield "hidden_local"
    loaded("own")
    receive("hs")

    def project(distance, half):
        block = (y + distance) % 8
        cc = c if half == 0 else 1 - c
        total = jnp.zeros((224, 128), F32)
        for b in range(4):
            zz = (zl + b) % 4
            weights = lt[zz // 2, cc, :, :, pl.ds(pl.multiple_of((zz % 2) * 256, 256), 256)].reshape(128, 256)
            total = total + lax.dot_general(
                hbuf[block, :, b * 256 : b * 256 + 256], weights,
                (((1,), (1,)), ((), ())), preferred_element_type=F32,
            )
        part[distance, half] = total

    def sum_copy(direction, half, step):
        sign = 1 - 2 * direction
        return rcopy(
            stage.at[direction, half, step], arrived.at[direction, half, step],
            rs_s.at[direction, half, step], rs_r.at[direction, half, step], at_y(sign * (2 if step == 0 else 1)),
        )

    def sum_send(direction, half, step):
        distance = 4 - step if direction == 0 else 4 + step
        value = part[distance, half]
        sources = [1] + ([0] if half == direction else []) if step == 2 else [2] if step == 3 else []
        for source in sources:
            receive(("sum", direction, half, source))
            value = value + arrived[direction, half, source].astype(F32)
        stage[direction, half, step] = value.astype(BF)
        copy = sum_copy(direction, half, step)
        send(copy)
        expect(("sum", direction, half, step), copy)

    yield "hidden_wait_0"
    hidden_wait(0)
    yield "sum_0"
    for half in (0, 1):
        if half == 1:
            for zz in range(4):
                receive(("lc", zz))
        project(4, half)
        sum_send(half, half, 0)
        project(3, half)
        sum_send(0, half, 1)
        project(5, half)
        sum_send(1, half, 1)
    yield "hidden_wait_1"
    hidden_wait(1)
    yield "sum_1"
    for half in (0, 1):
        project(2, half)
        project(6, half)
        sum_send(0, half, 2)
        sum_send(1, half, 2)
    core_send(0)
    yield "sum_2"
    for half in (0, 1):
        project(1, half)
        project(7, half)
        sum_send(0, half, 3)
        sum_send(1, half, 3)
    for half in (0, 1):
        project(0, half)

    row = lax.broadcasted_iota(jnp.int32, (256, 256), 0)
    column = lax.broadcasted_iota(jnp.int32, (256, 256), 1)
    swapped = (row // 128) * 32 + ((row // 64) % 2) * 64 + ((row // 32) % 2) * 128 + row % 32
    order = jnp.where(swapped == column, 1.0, 0.0).astype(BF)
    loaded("mom1")
    loaded("mom2")
    n1[...] = jnp.dot(m1[...], order, preferred_element_type=F32)
    n2[...] = jnp.dot(m2[...], order, preferred_element_type=F32)

    def gather_x(half, which, source, lanes):
        ref = dr.at[source, :, lanes]
        for k, (sx, dev) in enumerate(xpeers):
            send(rcopy(ref, ref, dx_s.at[half, which, k], dx_r.at[half, source], dev))
            peer = source - x + sx
            expect(("dx", half, which, k), landing(dr.at[peer, :, lanes], dx_r.at[half, peer]))

    other = (1 - zh) * 4 + x
    lane_sets = []
    for half in (0, 1):
        yield "sum_end_%d" % half
        value = part[0, half]
        for direction in (0, 1):
            receive(("sum", direction, half, 3))
            value = value + arrived[direction, half, 3].astype(F32)
        lanes = pl.ds(pl.multiple_of((c if half == 0 else 1 - c) * 128, 128), 128)
        lane_sets.append(lanes)
        first_f = 0.9 * n1[:, lanes] + 0.1 * value
        second_f = 0.999 * n2[:, lanes] + 0.001 * value * value
        dr[rank, :, lanes] = (first_f / FIRST_FIX / (jnp.sqrt(second_f / SECOND_FIX) + 1e-08)).astype(BF)
        send(rcopy(dr.at[rank, :, lanes], dr.at[rank, :, lanes], dz_s.at[half], dz_r.at[half], partner))
        expect(("dz", half), landing(dr.at[other, :, lanes], dz_r.at[half]))
        gather_x(half, 0, rank, lanes)
        n1[:, lanes] = first_f
        n2[:, lanes] = second_f

    m1[...] = jnp.dot(n1[...].astype(BF), order, preferred_element_type=F32).astype(BF)
    m2[...] = jnp.dot(n2[...].astype(BF), order, preferred_element_type=F32).astype(BF)
    load("new1", pltpu.make_async_copy(m1, new1, out_sem.at[4]))
    load("new2", pltpu.make_async_copy(m2, new2, out_sem.at[5]))
    yield "dir_z_wait"
    for half in (0, 1):
        receive(("dz", half))
        gather_x(half, 1, other, lane_sets[half])
    yield "rest"
    for k in range(7):
        receive(("p2", k))
    core_send(1)
    receive(("pc", 0))
    receive(("pc", 1))
    yield "dir_x_wait"

    def update(which, finish):
        for half in (0, 1):
            for k in range(3):
                receive(("dx", half, which, k))
        begin = (zh if which == 0 else 1 - zh) * 4

        def columns(n, carry):
            lanes = pl.ds(pl.multiple_of(n * 256, 256), 256)
            total = acc[n] if finish else jnp.zeros((224, 256), F32)
            for r in range(4):
                rows = p_t[begin + r, :, :, :, lanes].reshape(256, 256)
                total = total + jnp.dot(dr[begin + r], rows, preferred_element_type=F32)
            if finish:
                upd_v[:, lanes] = total.astype(BF)
                pltpu.make_async_copy(upd_v.at[:, lanes], upd.at[:, lanes], out_sem.at[n]).start()
            else:
                acc[n] = total
            return carry

        lax.fori_loop(0, 4, columns, 0)

    yield "update_0"
    update(0, False)
    yield "update_1"
    update(1, True)
    for n in range(4):
        lanes = pl.ds(n * 256, 256)
        pltpu.make_async_copy(upd_v.at[:, lanes], upd.at[:, lanes], out_sem.at[n]).wait()


def hand_over(*refs):
    sems = refs[9]
    reads = [pltpu.make_async_copy(refs[k], refs[6 + k], sems.at[0, k]) for k in range(3)]
    writes = [pltpu.make_async_copy(refs[6 + k], refs[3 + k], sems.at[1, k]) for k in range(3)]
    for copy in reads:
        copy.start()
    for read, write in zip(reads, writes):
        read.wait()
        write.start()
    for copy in writes:
        copy.wait()


def per_device(cotangents, hidden, projector, moment_first, moment_second):
    dma = pltpu.SemaphoreType.DMA
    anywhere = pl.BlockSpec(memory_space=pl.ANY)
    shapes = (
        jax.ShapeDtypeStruct((224, 1024), BF),
        jax.ShapeDtypeStruct((224, 256), BF),
        jax.ShapeDtypeStruct((224, 256), BF),
    )
    results = pl.pallas_call(
        kernel,
        out_shape=shapes,
        in_specs=[anywhere] * 5,
        out_specs=(anywhere, anywhere, anywhere),
        scratch_shapes=[
            pltpu.VMEM((128, 14336), BF),
            pltpu.VMEM((128, 1024), BF),
            pltpu.VMEM((8, 1792, 128), BF),
            pltpu.VMEM((8, 224, 1024), BF),
            pltpu.VMEM((8, 2, 2, 64, 1024), BF),
            pltpu.VMEM((1024, 512), BF),
            pltpu.VMEM((8, 64, 512), BF),
            pltpu.VMEM((4, 2, 64, 512), BF),
            pltpu.VMEM((64, 512), BF),
            pltpu.VMEM((64, 512), BF),
            pltpu.VMEM((2, 2, 2, 64, 512), BF),
            pltpu.VMEM((8, 2, 224, 128), F32),
            pltpu.VMEM((2, 2, 4, 224, 128), BF),
            pltpu.VMEM((2, 2, 4, 224, 128), BF),
            pltpu.VMEM((8, 224, 256), BF),
            pltpu.VMEM((224, 256), BF),
            pltpu.VMEM((224, 256), BF),
            pltpu.VMEM((224, 256), F32),
            pltpu.VMEM((224, 256), F32),
            pltpu.VMEM((4, 224, 256), F32),
            pltpu.VMEM((224, 1024), BF),
            dma((6,)),
            dma((6,)),
            dma((4,)), dma((4,)),
            dma((3,)), dma((3,)),
            dma((2, 2, 4)), dma((2, 2, 4)),
            dma((2, 3, 2)), dma((2, 6)),
            dma((2, 2, 3)), dma((2, 2, 3)),
            dma, dma,
            dma((8,)), dma((4, 2)),
            dma, dma,
            dma((3,)), dma((4,)),
            dma((4,)), dma((4,)),
            dma((7,)), dma((7,)),
            dma((2,)), dma((2,)),
            dma((2, 2, 4)), dma((2, 2, 4)),
            dma((2,)), dma((2,)),
            dma((2, 2, 3)), dma((2, 8)),
        ],
        compiler_params=pltpu.CompilerParams(
            collective_id=0, has_side_effects=True, vmem_limit_bytes=VL * 2**20
        ),
        cost_estimate=pl.CostEstimate(flops=2_500_000_000, bytes_accessed=6_000_000, transcendentals=60_000),
        name="galore",
    )(cotangents, hidden, projector.T, moment_first.T, moment_second.T)
    results = pl.pallas_call(
        hand_over,
        out_shape=shapes,
        in_specs=[anywhere] * 3,
        out_specs=(anywhere,) * 3,
        scratch_shapes=[pltpu.VMEM(shape.shape, BF) for shape in shapes] + [dma((2, 3))],
        cost_estimate=pl.CostEstimate(flops=0, bytes_accessed=1_400_000, transcendentals=0),
        name="hand_over",
    )(*results)
    return tuple(array.T for array in results)


def solution(mesh):
    return jax.shard_map(
        per_device,
        mesh=mesh,
        in_specs=(
            P("fsdp", "rank"),
            P("fsdp", None),
            P("rank", "fsdp"),
            P("rank", "fsdp"),
            P("rank", "fsdp"),
        ),
        out_specs=(P("rank", "fsdp"), P("rank", "fsdp"), P("rank", "fsdp")),
        check_vma=False,
    )
```
